256 devices in a mesh: tensor: 4 (over y), context: 64 (over x, z, core).
Axes of the slice: x: 4, y: 4, z: 8, core: 2. Of those that a mesh axis runs over, the one named last changes fastest.
Arguments:
- query_gate: bfloat16 [8192, 4096], P('context', 'tensor'), may hold values from -6 to 6
- key_gate: bfloat16 [8192, 4096], P('context', 'tensor'), may hold values from -6 to 6
- value_in: bfloat16 [8192, 4096], P('context', 'tensor'), may hold values from -6 to 6
- filter_raw: float32 [8192, 256], P('context', 'tensor'), may hold values from -6 to 6
- grad_out: bfloat16 [8192, 4096], P('context', 'tensor'), may hold values from -6 to 6
Outputs:
- output: bfloat16 [8192, 4096], P('context', 'tensor')
- grad_query: bfloat16 [8192, 4096], P('context', 'tensor')
- grad_key: bfloat16 [8192, 4096], P('context', 'tensor')
- grad_value: bfloat16 [8192, 4096], P('context', 'tensor')
- grad_filter: float32 [8192, 256], P('context', 'tensor')
The draws below stay inside these ranges and needn't reach their ends.
All inputs are finite; a program needn't handle non-finite values.
Results may differ from the reference program's by a relative error of at most 0.0011.
Values sent between devices are 32-bit elements; how exact they have to be, the bound alone decides.
No kernel may reach another device: no remote copies, remote signals or barrier semaphores. Data moves between devices by JAX's collectives and lax.ppermute only.
A program may use at most 64 MiB of HBM per device.

```python
import math
import jax
import jax.numpy as jnp
from jax import lax

CH_DEV = 1024
GROUP = 16
SEQ = 8192
CHANNELS = 4096
FILT_DEV = 64
FILTERS = 256
N_TENSOR = 4


def block_scale(stream_key, shape, shards, least, largest):
    factor_of, own = 1.0, jax.random.fold_in(stream_key, 6)
    for position, blocks in shards:
        steps = jnp.exp(jax.random.uniform(jax.random.fold_in(own, position), (blocks,), jnp.float32, least / len(shards), largest / len(shards)))
        factor_of = factor_of * jnp.repeat(steps, shape[position] // blocks).reshape([-1 if axis == position else 1 for axis in range(len(shape))])
    return factor_of


def centred(key, shape, deviation, reach, split=(), held_as=jnp.bfloat16):
    loudness = block_scale(key, shape, split, -0.22, 0.18) if split else 1.0
    result = jax.random.normal(key, shape, jnp.float32) * deviation * loudness
    return jnp.minimum(jnp.maximum(result, -reach), reach).astype(held_as)


def setup_inputs(seed: int = 0) -> dict:
    splits = jax.random.split(jax.random.key(seed), 6)
    return {
        "query_gate": centred(splits[0], (SEQ, CHANNELS), 1.0, 6.0, ((0, 64), (1, 4))),
        "key_gate": centred(splits[1], (SEQ, CHANNELS), 1.0, 6.0, ((0, 64), (1, 4))),
        "value_in": centred(splits[2], (SEQ, CHANNELS), 1.0, 6.0, ((0, 64), (1, 4))),
        "filter_raw": centred(splits[3], (SEQ, FILTERS), 1.0, 6.0, ((0, 64), (1, 4)), jnp.float32),
        "grad_out": centred(splits[4], (SEQ, CHANNELS), 1.0, 6.0, ((0, 64), (1, 4))),
    }


def one_slab(pieces):
    query_gate, key_gate, value_in, filter_raw, grad_out = pieces
    points = 2 * SEQ
    scale = 1.0 / math.sqrt(SEQ)
    query_full = query_gate.astype(jnp.float32)
    key_full = key_gate.astype(jnp.float32)
    value_full = value_in.astype(jnp.float32)
    grad_full = grad_out.astype(jnp.float32)
    gated = key_full * value_full
    filt = jnp.repeat(filter_raw.astype(jnp.float32) * scale, GROUP, axis=1)
    spec_gated = jnp.fft.rfft(gated, n=points, axis=0)
    spec_filt = jnp.fft.rfft(filt, n=points, axis=0)
    grad_conv = grad_full * query_full
    spec_grad = jnp.fft.rfft(grad_conv, n=points, axis=0)
    conv = jnp.fft.irfft(spec_gated * spec_filt, n=points, axis=0)[:SEQ]
    grad_gated = jnp.fft.irfft(jnp.conj(spec_filt) * spec_grad, n=points, axis=0)[:SEQ]
    corr = jnp.fft.irfft(jnp.conj(spec_gated) * spec_grad, n=points, axis=0)[:SEQ]
    output = (query_full * conv).astype(jnp.bfloat16)
    grad_query = (grad_full * conv).astype(jnp.bfloat16)
    grad_key = (grad_gated * value_full).astype(jnp.bfloat16)
    grad_value = (grad_gated * key_full).astype(jnp.bfloat16)
    grad_filter = (lax.optimization_barrier(jnp.sum(corr.reshape(SEQ, FILT_DEV, GROUP), axis=2)) * scale).astype(jnp.float32)
    return (output, grad_query, grad_key, grad_value, grad_filter)

def split_slabs(array, count):
    return jnp.transpose(array.reshape(SEQ, N_TENSOR, count), (1, 0, 2))

def join_slabs(array):
    return jnp.transpose(array, (1, 0, 2)).reshape(SEQ, -1)

def reference(query_gate, key_gate, value_in, filter_raw, grad_out):
    pieces = (split_slabs(query_gate, CH_DEV), split_slabs(key_gate, CH_DEV), split_slabs(value_in, CH_DEV), split_slabs(filter_raw, FILT_DEV), split_slabs(grad_out, CH_DEV))
    results = lax.map(one_slab, pieces)
    return (join_slabs(results[0]), join_slabs(results[1]), join_slabs(results[2]), join_slabs(results[3]), join_slabs(results[4]))
```

```python
import math

import jax
import jax.numpy as jnp
import ml_dtypes
import numpy as np
from jax import lax
from jax.experimental import pallas as pl
from jax.experimental.pallas import tpu as pltpu
from jax.sharding import PartitionSpec as P

bf16 = jnp.bfloat16
f32 = jnp.float32


def split_table(table):
    high = table.astype(np.float32).astype(ml_dtypes.bfloat16)
    low = (table - high.astype(np.float64)).astype(np.float32).astype(ml_dtypes.bfloat16)
    return high, low


def tables(blocks, inner, scale):
    points = 2 * blocks * inner
    a = np.arange(blocks)
    b = np.arange(inner)
    odd = 2 * np.arange(blocks) + 1
    across = np.pi * np.outer(odd, a) / (2 * blocks)
    fore = np.concatenate([np.cos(across), -np.sin(across)], axis=0)
    back = np.concatenate([np.cos(across), -np.sin(across)], axis=0).T
    fore_high, fore_low = split_table(fore)
    back_high, back_low = split_table(back)
    turn = np.pi * np.outer(odd, b) / points
    turn_fore = np.stack([np.cos(turn), -np.sin(turn)]).astype(np.float32)
    turn_back = (np.stack([np.cos(turn), np.sin(turn)]) * (2.0 * scale / points)).astype(np.float32)
    within = 2 * np.pi * np.outer(b, b) / inner
    cosine, sine = np.cos(within), np.sin(within)
    wide_fore = np.block([[cosine, -sine], [sine, cosine]])
    wide_back = np.block([[cosine, sine], [-sine, cosine]])
    fh, fl = split_table(wide_fore)
    bh, bl = split_table(wide_back)
    return (
        np.concatenate([fore_high, fore_high, fore_low], axis=1),
        np.concatenate([back_high, back_high, back_low], axis=1),
        np.concatenate([fh, fh, fl], axis=0),
        np.concatenate([bh, bh, bl], axis=0),
        turn_fore,
        turn_back,
    )


def halves(value):
    high = value.astype(bf16)
    return high, (value - high.astype(f32)).astype(bf16)


def dot(left, right):
    return jnp.dot(left, right, preferred_element_type=f32)


def pack_kernel(peers, lanes, query_ref, key_ref, value_ref, filter_ref, grad_ref, out_ref, turned_ref):
    rows = 2 * lanes + 1
    width = peers * lanes
    for index, (left, right) in enumerate(((key_ref, value_ref), (grad_ref, query_ref))):
        for start in range(0, width, 128):
            part = pl.ds(start, 128)
            product = left[:, part].astype(f32) * right[:, part].astype(f32)
            turned_ref[pl.ds(index * width + start, 128), :] = product.T
    for index in range(2):
        for lane in range(lanes):
            out_ref[pl.ds(index * lanes + lane, peers, stride=rows), :] = turned_ref[
                pl.ds(index * width + lane, peers, stride=lanes), :
            ]
    out_ref[pl.ds(2 * lanes, peers, stride=rows), :] = filter_ref[...].T


def convolve_kernel(
    peers,
    lanes,
    in_ref,
    fore_ref,
    back_ref,
    wide_fore_ref,
    wide_back_ref,
    turn_fore_ref,
    turn_back_ref,
    out_ref,
    high_ref,
    low_ref,
):
    rows = 2 * lanes + 1
    inner = in_ref.shape[1]
    chunk = 4

    def place(first, count=1):
        return pl.ds(first * peers, count * peers)

    def put(first, value):
        high, low = halves(value)
        here = pl.ds(first * peers, value.shape[0])
        high_ref[here, :] = high
        low_ref[here, :] = low

    def transformed(first, count, table_ref):
        high = high_ref[place(first, count), :]
        low = low_ref[place(first, count), :]
        return dot(jnp.concatenate([high, low, high], axis=1), table_ref[...])

    def rotated(real, imag, turn_ref):
        cosine, sine = turn_ref[0], turn_ref[1]
        return jnp.concatenate(
            [real * cosine - imag * sine, real * sine + imag * cosine], axis=1
        )

    fore = fore_ref[...]
    order = [2 * lanes] + list(range(2 * lanes))
    for start in range(0, rows, 2):
        chosen = order[start : start + 2]
        columns = []
        for row in chosen:
            high, low = halves(in_ref[pl.ds(row, peers, stride=rows), :])
            columns.append(jnp.concatenate([high, low, high], axis=0))
        spread = dot(fore, jnp.concatenate(columns, axis=1))
        for index, row in enumerate(chosen):
            part = spread[:, index * inner : (index + 1) * inner]
            put(row, rotated(part[:peers], part[peers:], turn_fore_ref))

    filt = transformed(2 * lanes, 1, wide_fore_ref)
    filt_re, filt_im = filt[:, :inner], filt[:, inner:]
    corr_re = jnp.zeros((peers, inner), f32)
    corr_im = jnp.zeros((peers, inner), f32)
    for first in range(0, lanes, chunk):
        gated = transformed(first, chunk, wide_fore_ref)
        grad = transformed(lanes + first, chunk, wide_fore_ref)
        for index in range(chunk):
            part = slice(index * peers, (index + 1) * peers)
            gated_re, gated_im = gated[part, :inner], gated[part, inner:]
            grad_re, grad_im = grad[part, :inner], grad[part, inner:]
            put(
                first + index,
                jnp.concatenate(
                    [
                        gated_re * filt_re - gated_im * filt_im,
                        gated_re * filt_im + gated_im * filt_re,
                    ],
                    axis=1,
                ),
            )
            put(
                lanes + first + index,
                jnp.concatenate(
                    [
                        filt_re * grad_re + filt_im * grad_im,
                        filt_re * grad_im - filt_im * grad_re,
                    ],
                    axis=1,
                ),
            )
            corr_re = corr_re + (gated_re * grad_re + gated_im * grad_im)
            corr_im = corr_im + (gated_re * grad_im - gated_im * grad_re)
    put(2 * lanes, jnp.concatenate([corr_re, corr_im], axis=1))

    back = back_ref[...]
    for first in range(0, rows, chunk):
        count = min(chunk, rows - first)
        spec = transformed(first, count, wide_back_ref)
        for start in range(0, count, 2):
            columns = []
            for index in range(start, min(start + 2, count)):
                part = spec[index * peers : (index + 1) * peers]
                turned = rotated(part[:, :inner], part[:, inner:], turn_back_ref)
                stacked = jnp.concatenate([turned[:, :inner], turned[:, inner:]], axis=0)
                high, low = halves(stacked)
                columns.append(jnp.concatenate([high, low, high], axis=0))
            signal = dot(back, jnp.concatenate(columns, axis=1))
            for index in range(len(columns)):
                out_ref[pl.ds(first + start + index, peers, stride=rows), :] = signal[
                    :, index * inner : (index + 1) * inner
                ]


def unpack_kernel(
    peers,
    lanes,
    in_ref,
    query_ref,
    key_ref,
    value_ref,
    grad_ref,
    output_ref,
    grad_query_ref,
    grad_key_ref,
    grad_value_ref,
    grad_filter_ref,
    turned_ref,
):
    rows = 2 * lanes + 1
    width = peers * lanes
    for index in range(2):
        for lane in range(lanes):
            turned_ref[pl.ds(index * width + lane, peers, stride=lanes), :] = in_ref[
                pl.ds(index * lanes + lane, peers, stride=rows), :
            ]
    for start in range(0, width, 128):
        part = pl.ds(start, 128)
        conv = turned_ref[part, :].T
        output_ref[:, part] = (query_ref[:, part].astype(f32) * conv).astype(bf16)
        grad_query_ref[:, part] = (grad_ref[:, part].astype(f32) * conv).astype(bf16)
        grad_gated = turned_ref[pl.ds(width + start, 128), :].T
        grad_key_ref[:, part] = (grad_gated * value_ref[:, part].astype(f32)).astype(bf16)
        grad_value_ref[:, part] = (grad_gated * key_ref[:, part].astype(f32)).astype(bf16)
    grad_filter_ref[...] = in_ref[pl.ds(2 * lanes, peers, stride=rows), :].T


def exchange(signal, rows):
    pieces = signal.reshape(signal.shape[0], 1, signal.shape[1])
    pieces = lax.all_to_all(pieces, "context", 0, 0, tiled=True)
    return pieces.reshape(signal.shape)


def solution(mesh):
    peers = mesh.shape["context"]
    params = pltpu.CompilerParams(vmem_limit_bytes=48 * 1024 * 1024)

    def local(query_gate, key_gate, value_in, filter_raw, grad_out):
        inner, width = query_gate.shape
        lanes = width // filter_raw.shape[1]
        rows = 2 * lanes + 1
        scale = 1.0 / math.sqrt(peers * inner)
        packed = jax.ShapeDtypeStruct((peers * rows, inner), f32)
        turned = pltpu.VMEM((2 * width, inner), f32)
        sent = pl.pallas_call(
            lambda *refs: pack_kernel(peers, lanes, *refs),
            out_shape=packed,
            scratch_shapes=[turned],
            compiler_params=params,
            name="pack",
        )(query_gate, key_gate, value_in, filter_raw, grad_out)
        held = exchange(sent, rows)
        result = pl.pallas_call(
            lambda *refs: convolve_kernel(peers, lanes, *refs),
            out_shape=packed,
            scratch_shapes=[pltpu.VMEM((peers * rows, 2 * inner), bf16)] * 2,
            compiler_params=params,
            name="convolve",
        )(held, *(jnp.asarray(table) for table in tables(peers, inner, scale)))
        back = exchange(result, rows)
        wide = jax.ShapeDtypeStruct((inner, width), bf16)
        return pl.pallas_call(
            lambda *refs: unpack_kernel(peers, lanes, *refs),
            out_shape=(wide, wide, wide, wide, jax.ShapeDtypeStruct(filter_raw.shape, f32)),
            scratch_shapes=[turned],
            compiler_params=params,
            name="unpack",
        )(back, query_gate, key_gate, value_in, grad_out)

    spec = P("context", "tensor")
    return jax.shard_map(
        local, mesh=mesh, in_specs=(spec,) * 5, out_specs=(spec,) * 5, check_vma=False
    )
```

```python
import math

import jax
import jax.numpy as jnp
import ml_dtypes
import numpy as np
from jax import lax
from jax.experimental import pallas as pl
from jax.experimental.pallas import tpu as pltpu
from jax.sharding import PartitionSpec as P

bf16 = jnp.bfloat16
f32 = jnp.float32


def split_table(table):
    high = table.astype(np.float32).astype(ml_dtypes.bfloat16)
    low = (table - high.astype(np.float64)).astype(np.float32).astype(ml_dtypes.bfloat16)
    return high, low


def tables(blocks, inner, scale):
    points = 2 * blocks * inner
    a = np.arange(blocks)
    b = np.arange(inner)
    odd = 2 * np.arange(blocks) + 1
    across = np.pi * np.outer(odd, a) / (2 * blocks)
    fore = np.concatenate([np.cos(across), -np.sin(across)], axis=0)
    back = np.concatenate([np.cos(across), -np.sin(across)], axis=0).T
    fore_high, fore_low = split_table(fore)
    back_high, back_low = split_table(back)
    turn = np.pi * np.outer(odd, b) / points
    turn_fore = np.stack([np.cos(turn), -np.sin(turn)]).astype(np.float32)
    turn_back = (np.stack([np.cos(turn), np.sin(turn)]) * (2.0 * scale / points)).astype(np.float32)
    within = 2 * np.pi * np.outer(b, b) / inner
    cosine, sine = np.cos(within), np.sin(within)
    wide_fore = np.block([[cosine, -sine], [sine, cosine]])
    wide_back = np.block([[cosine, sine], [-sine, cosine]])
    fh, fl = split_table(wide_fore)
    bh, bl = split_table(wide_back)
    return (
        np.concatenate([fore_high, fore_high, fore_low], axis=1),
        np.concatenate([back_high, back_high, back_low], axis=1),
        np.concatenate([fh, fh, fl], axis=0),
        np.concatenate([bh, bh, bl], axis=0),
        turn_fore,
        turn_back,
    )


def halves(value):
    high = value.astype(bf16)
    return high, (value - high.astype(f32)).astype(bf16)


def dot(left, right):
    return jnp.dot(left, right, preferred_element_type=f32)


def pack_kernel(
    peers,
    lanes,
    parts,
    query_hbm,
    key_hbm,
    value_hbm,
    filter_hbm,
    grad_hbm,
    out_ref,
    query_ref,
    key_ref,
    value_ref,
    grad_ref,
    filter_ref,
    turned_ref,
    sems,
):
    rows = 2 * lanes + 1
    width = peers * lanes
    span = width // parts
    pairs = (
        ((key_hbm, key_ref), (value_hbm, value_ref)),
        ((grad_hbm, grad_ref), (query_hbm, query_ref)),
    )
    copies = {}
    for index, pair in enumerate(pairs):
        for part in range(parts):
            for side, (source, target) in enumerate(pair):
                columns = pl.ds(part * span, span)
                copy = pltpu.make_async_copy(
                    source.at[:, columns], target.at[:, columns], sems.at[index, side, part]
                )
                copy.start()
                copies[index, side, part] = copy
    filter_copy = pltpu.make_async_copy(filter_hbm, filter_ref, sems.at[2, 0, 0])
    filter_copy.start()
    for index, ((_, left), (_, right)) in enumerate(pairs):
        for part in range(parts):
            copies[index, 0, part].wait()
            copies[index, 1, part].wait()
            for start in range(part * span, (part + 1) * span, 128):
                columns = pl.ds(start, 128)
                product = left[:, columns].astype(f32) * right[:, columns].astype(f32)
                turned_ref[pl.ds(index * width + start, 128), :] = product.T
        for lane in range(lanes):
            out_ref[pl.ds(index * lanes + lane, peers, stride=rows), :] = turned_ref[
                pl.ds(index * width + lane, peers, stride=lanes), :
            ]
    filter_copy.wait()
    out_ref[pl.ds(2 * lanes, peers, stride=rows), :] = filter_ref[...]


def convolve_kernel(
    peers,
    lanes,
    in_ref,
    fore_ref,
    back_ref,
    wide_fore_ref,
    wide_back_ref,
    turn_fore_ref,
    turn_back_ref,
    out_ref,
    high_ref,
    low_ref,
):
    rows = 2 * lanes + 1
    inner = in_ref.shape[1]
    chunk = 4

    def place(first, count=1):
        return pl.ds(first * peers, count * peers)

    def put(first, value):
        high, low = halves(value)
        here = pl.ds(first * peers, value.shape[0])
        high_ref[here, :] = high
        low_ref[here, :] = low

    def transformed(first, count, table_ref):
        high = high_ref[place(first, count), :]
        low = low_ref[place(first, count), :]
        return dot(jnp.concatenate([high, low, high], axis=1), table_ref[...])

    def rotated(real, imag, turn_ref):
        cosine, sine = turn_ref[0], turn_ref[1]
        return jnp.concatenate(
            [real * cosine - imag * sine, real * sine + imag * cosine], axis=1
        )

    fore = fore_ref[...]
    order = [2 * lanes] + list(range(2 * lanes))
    for start in range(0, rows, 2):
        chosen = order[start : start + 2]
        columns = []
        for row in chosen:
            high, low = halves(in_ref[pl.ds(row, peers, stride=rows), :])
            columns.append(jnp.concatenate([high, low, high], axis=0))
        spread = dot(fore, jnp.concatenate(columns, axis=1))
        for index, row in enumerate(chosen):
            part = spread[:, index * inner : (index + 1) * inner]
            put(row, rotated(part[:peers], part[peers:], turn_fore_ref))

    filt = transformed(2 * lanes, 1, wide_fore_ref)
    filt_re, filt_im = filt[:, :inner], filt[:, inner:]
    corr_re = jnp.zeros((peers, inner), f32)
    corr_im = jnp.zeros((peers, inner), f32)
    for first in range(0, lanes, chunk):
        gated = transformed(first, chunk, wide_fore_ref)
        grad = transformed(lanes + first, chunk, wide_fore_ref)
        for index in range(chunk):
            part = slice(index * peers, (index + 1) * peers)
            gated_re, gated_im = gated[part, :inner], gated[part, inner:]
            grad_re, grad_im = grad[part, :inner], grad[part, inner:]
            put(
                first + index,
                jnp.concatenate(
                    [
                        gated_re * filt_re - gated_im * filt_im,
                        gated_re * filt_im + gated_im * filt_re,
                    ],
                    axis=1,
                ),
            )
            put(
                lanes + first + index,
                jnp.concatenate(
                    [
                        filt_re * grad_re + filt_im * grad_im,
                        filt_re * grad_im - filt_im * grad_re,
                    ],
                    axis=1,
                ),
            )
            corr_re = corr_re + (gated_re * grad_re + gated_im * grad_im)
            corr_im = corr_im + (gated_re * grad_im - gated_im * grad_re)
    put(2 * lanes, jnp.concatenate([corr_re, corr_im], axis=1))

    for first in range(0, rows, chunk):
        count = min(chunk, rows - first)
        spec = transformed(first, count, wide_back_ref)
        for index in range(count):
            part = spec[index * peers : (index + 1) * peers]
            put(first + index, rotated(part[:, :inner], part[:, inner:], turn_back_ref))

    back = back_ref[...]
    for start in range(0, rows, 2):
        columns = []
        for row in range(start, min(start + 2, rows)):
            high, low = high_ref[place(row), :], low_ref[place(row), :]
            high = jnp.concatenate([high[:, :inner], high[:, inner:]], axis=0)
            low = jnp.concatenate([low[:, :inner], low[:, inner:]], axis=0)
            columns.append(jnp.concatenate([high, low, high], axis=0))
        signal = dot(back, jnp.concatenate(columns, axis=1))
        for index in range(len(columns)):
            out_ref[pl.ds(start + index, peers, stride=rows), :] = signal[
                :, index * inner : (index + 1) * inner
            ]


def unpack_kernel(
    peers,
    lanes,
    parts,
    in_ref,
    query_ref,
    key_ref,
    value_ref,
    grad_ref,
    output_hbm,
    grad_query_hbm,
    grad_key_hbm,
    grad_value_hbm,
    grad_filter_hbm,
    output_ref,
    grad_query_ref,
    grad_key_ref,
    grad_value_ref,
    grad_filter_ref,
    turned_ref,
    sems,
):
    rows = 2 * lanes + 1
    width = peers * lanes
    span = width // parts
    grad_filter_ref[...] = in_ref[pl.ds(2 * lanes, peers, stride=rows), :]
    copies = [pltpu.make_async_copy(grad_filter_ref, grad_filter_hbm, sems.at[4, 0])]
    copies[0].start()
    sides = (
        (
            (query_ref, output_ref, output_hbm),
            (grad_ref, grad_query_ref, grad_query_hbm),
        ),
        (
            (value_ref, grad_key_ref, grad_key_hbm),
            (key_ref, grad_value_ref, grad_value_hbm),
        ),
    )
    for index, pair in enumerate(sides):
        for lane in range(lanes):
            turned_ref[pl.ds(index * width + lane, peers, stride=lanes), :] = in_ref[
                pl.ds(index * lanes + lane, peers, stride=rows), :
            ]
        for part in range(parts):
            for start in range(part * span, (part + 1) * span, 128):
                columns = pl.ds(start, 128)
                signal = turned_ref[pl.ds(index * width + start, 128), :].T
                for factor, target, _ in pair:
                    target[:, columns] = (factor[:, columns].astype(f32) * signal).astype(bf16)
            columns = pl.ds(part * span, span)
            for side, (_, source, target) in enumerate(pair):
                copy = pltpu.make_async_copy(
                    source.at[:, columns], target.at[:, columns], sems.at[2 * index + side, part]
                )
                copy.start()
                copies.append(copy)
    for copy in copies:
        copy.wait()


def exchange(signal):
    pieces = signal.reshape(signal.shape[0], 1, signal.shape[1])
    pieces = lax.all_to_all(pieces, "context", 0, 0, tiled=True)
    return pieces.reshape(signal.shape)


def solution(mesh):
    peers = mesh.shape["context"]
    params = pltpu.CompilerParams(vmem_limit_bytes=48 * 1024 * 1024)

    def local(query_gate, key_gate, value_in, filter_raw, grad_out):
        inner, width = query_gate.shape
        lanes = width // filter_raw.shape[1]
        rows = 2 * lanes + 1
        scale = 1.0 / math.sqrt(peers * inner)
        packed = jax.ShapeDtypeStruct((peers * rows, inner), f32)
        turned = pltpu.VMEM((2 * width, inner), f32)
        held_wide = pltpu.VMEM((inner, width), bf16)
        held_filter = pltpu.VMEM((peers, inner), f32)
        parts = 4
        sent = pl.pallas_call(
            lambda *refs: pack_kernel(peers, lanes, parts, *refs),
            out_shape=packed,
            in_specs=[pl.BlockSpec(memory_space=pltpu.HBM)] * 5,
            scratch_shapes=[held_wide] * 4
            + [held_filter, turned, pltpu.SemaphoreType.DMA((3, 2, parts))],
            compiler_params=params,
            name="pack",
        )(
            *(
                pltpu.with_memory_space_constraint(array, pltpu.HBM)
                for array in (query_gate, key_gate, value_in, filter_raw.T, grad_out)
            )
        )
        held = exchange(sent)
        result = pl.pallas_call(
            lambda *refs: convolve_kernel(peers, lanes, *refs),
            out_shape=packed,
            scratch_shapes=[pltpu.VMEM((peers * rows, 2 * inner), bf16)] * 2,
            compiler_params=params,
            name="convolve",
        )(held, *(jnp.asarray(table) for table in tables(peers, inner, scale)))
        back = exchange(result)
        wide = jax.ShapeDtypeStruct((inner, width), bf16)
        *outputs, grad_filter = pl.pallas_call(
            lambda *refs: unpack_kernel(peers, lanes, parts, *refs),
            out_shape=(wide,) * 4 + (jax.ShapeDtypeStruct((peers, inner), f32),),
            out_specs=(pl.BlockSpec(memory_space=pltpu.HBM),) * 5,
            scratch_shapes=[held_wide] * 4
            + [held_filter, turned, pltpu.SemaphoreType.DMA((5, parts))],
            compiler_params=params,
            name="unpack",
        )(back, query_gate, key_gate, value_in, grad_out)
        return (*outputs, grad_filter.T)

    spec = P("context", "tensor")
    return jax.shard_map(
        local, mesh=mesh, in_specs=(spec,) * 5, out_specs=(spec,) * 5, check_vma=False
    )
```

```python
import math

import jax
import jax.numpy as jnp
import ml_dtypes
import numpy as np
from jax import lax
from jax.experimental import pallas as pl
from jax.experimental.pallas import tpu as pltpu
from jax.sharding import PartitionSpec as P

bf16 = jnp.bfloat16
f32 = jnp.float32


def split_table(table):
    high = table.astype(np.float32).astype(ml_dtypes.bfloat16)
    low = (table - high.astype(np.float64)).astype(np.float32).astype(ml_dtypes.bfloat16)
    return high, low


def tables(blocks, inner, scale):
    points = 2 * blocks * inner
    a = np.arange(blocks)
    b = np.arange(inner)
    odd = 2 * np.arange(blocks) + 1
    across = np.pi * np.outer(odd, a) / (2 * blocks)
    fore = np.concatenate([np.cos(across), -np.sin(across)], axis=0)
    back = np.concatenate([np.cos(across), -np.sin(across)], axis=0).T
    fore_high, fore_low = split_table(fore)
    back_high, back_low = split_table(back)
    turn = np.pi * np.outer(odd, b) / points
    turn_fore = np.stack([np.cos(turn), -np.sin(turn)]).astype(np.float32)
    turn_back = (np.stack([np.cos(turn), np.sin(turn)]) * (2.0 * scale / points)).astype(np.float32)
    within = 2 * np.pi * np.outer(b, b) / inner
    cosine, sine = np.cos(within), np.sin(within)
    wide_fore = np.block([[cosine, -sine], [sine, cosine]])
    wide_back = np.block([[cosine, sine], [-sine, cosine]])
    fh, fl = split_table(wide_fore)
    bh, bl = split_table(wide_back)
    return (
        np.concatenate([fore_high, fore_high, fore_low], axis=1),
        np.concatenate([back_high, back_high, back_low], axis=1),
        np.concatenate([fh, fh, fl], axis=0),
        np.concatenate([bh, bh, bl], axis=0),
        turn_fore,
        turn_back,
    )


def halves(value):
    high = value.astype(bf16)
    return high, (value - high.astype(f32)).astype(bf16)


def dot(left, right):
    return jnp.dot(left, right, preferred_element_type=f32)


def pack_kernel(
    peers,
    lanes,
    parts,
    query_hbm,
    key_hbm,
    value_hbm,
    filter_hbm,
    grad_hbm,
    out_ref,
    query_ref,
    key_ref,
    value_ref,
    grad_ref,
    filter_ref,
    sems,
):
    rows = 2 * lanes + 1
    width = peers * lanes
    span = width // parts
    pairs = (
        ((key_hbm, key_ref), (value_hbm, value_ref)),
        ((grad_hbm, grad_ref), (query_hbm, query_ref)),
    )
    copies = {}
    for index, pair in enumerate(pairs):
        for part in range(parts):
            for side, (source, target) in enumerate(pair):
                columns = pl.ds(part * span, span)
                copy = pltpu.make_async_copy(
                    source.at[:, columns], target.at[:, columns], sems.at[index, side, part]
                )
                copy.start()
                copies[index, side, part] = copy
    filter_copy = pltpu.make_async_copy(filter_hbm, filter_ref, sems.at[2, 0, 0])
    filter_copy.start()
    for index, ((_, left), (_, right)) in enumerate(pairs):
        for part in range(parts):
            copies[index, 0, part].wait()
            copies[index, 1, part].wait()
            for start in range(part * span, (part + 1) * span, 128):
                columns = pl.ds(start, 128)
                product = left[:, columns].astype(f32) * right[:, columns].astype(f32)
                turned = product.T
                for offset in range(0, 128, lanes):
                    first = (start + offset) // lanes * rows + index * lanes
                    out_ref[pl.ds(first, lanes), :] = turned[offset : offset + lanes]
    filter_copy.wait()
    out_ref[pl.ds(2 * lanes, peers, stride=rows), :] = filter_ref[...]


def convolve_kernel(
    peers,
    lanes,
    in_ref,
    fore_ref,
    back_ref,
    wide_fore_ref,
    wide_back_ref,
    turn_fore_ref,
    turn_back_ref,
    out_ref,
    high_ref,
    low_ref,
):
    rows = 2 * lanes + 1
    inner = in_ref.shape[1]
    chunk = 4

    def place(first, count=1):
        return pl.ds(first * peers, count * peers)

    def put(first, value):
        high, low = halves(value)
        here = pl.ds(first * peers, value.shape[0])
        high_ref[here, :] = high
        low_ref[here, :] = low

    def transformed(first, count, table_ref):
        high = high_ref[place(first, count), :]
        low = low_ref[place(first, count), :]
        return dot(jnp.concatenate([high, low, high], axis=1), table_ref[...])

    def rotated(real, imag, turn_ref):
        cosine, sine = turn_ref[0], turn_ref[1]
        return jnp.concatenate(
            [real * cosine - imag * sine, real * sine + imag * cosine], axis=1
        )

    fore = fore_ref[...]
    order = [2 * lanes] + list(range(2 * lanes))
    for start in range(0, rows, 2):
        chosen = order[start : start + 2]
        columns = []
        for row in chosen:
            high, low = halves(in_ref[pl.ds(row, peers, stride=rows), :])
            columns.append(jnp.concatenate([high, low, high], axis=0))
        spread = dot(fore, jnp.concatenate(columns, axis=1))
        for index, row in enumerate(chosen):
            part = spread[:, index * inner : (index + 1) * inner]
            put(row, rotated(part[:peers], part[peers:], turn_fore_ref))

    filt = transformed(2 * lanes, 1, wide_fore_ref)
    filt_re, filt_im = filt[:, :inner], filt[:, inner:]
    corr_re = jnp.zeros((peers, inner), f32)
    corr_im = jnp.zeros((peers, inner), f32)
    for first in range(0, lanes, chunk):
        gated = transformed(first, chunk, wide_fore_ref)
        grad = transformed(lanes + first, chunk, wide_fore_ref)
        for index in range(chunk):
            part = slice(index * peers, (index + 1) * peers)
            gated_re, gated_im = gated[part, :inner], gated[part, inner:]
            grad_re, grad_im = grad[part, :inner], grad[part, inner:]
            put(
                first + index,
                jnp.concatenate(
                    [
                        gated_re * filt_re - gated_im * filt_im,
                        gated_re * filt_im + gated_im * filt_re,
                    ],
                    axis=1,
                ),
            )
            put(
                lanes + first + index,
                jnp.concatenate(
                    [
                        filt_re * grad_re + filt_im * grad_im,
                        filt_re * grad_im - filt_im * grad_re,
                    ],
                    axis=1,
                ),
            )
            corr_re = corr_re + (gated_re * grad_re + gated_im * grad_im)
            corr_im = corr_im + (gated_re * grad_im - gated_im * grad_re)
    put(2 * lanes, jnp.concatenate([corr_re, corr_im], axis=1))

    for first in range(0, rows, chunk):
        count = min(chunk, rows - first)
        spec = transformed(first, count, wide_back_ref)
        for index in range(count):
            part = spec[index * peers : (index + 1) * peers]
            put(first + index, rotated(part[:, :inner], part[:, inner:], turn_back_ref))

    back = back_ref[...]
    for start in range(0, rows, 2):
        columns = []
        for row in range(start, min(start + 2, rows)):
            high, low = high_ref[place(row), :], low_ref[place(row), :]
            high = jnp.concatenate([high[:, :inner], high[:, inner:]], axis=0)
            low = jnp.concatenate([low[:, :inner], low[:, inner:]], axis=0)
            columns.append(jnp.concatenate([high, low, high], axis=0))
        signal = dot(back, jnp.concatenate(columns, axis=1))
        for index in range(len(columns)):
            out_ref[pl.ds(start + index, peers, stride=rows), :] = signal[
                :, index * inner : (index + 1) * inner
            ]


def unpack_kernel(
    peers,
    lanes,
    parts,
    in_ref,
    query_ref,
    key_ref,
    value_ref,
    grad_ref,
    output_hbm,
    grad_query_hbm,
    grad_key_hbm,
    grad_value_hbm,
    grad_filter_hbm,
    output_ref,
    grad_query_ref,
    grad_key_ref,
    grad_value_ref,
    grad_filter_ref,
    sems,
):
    rows = 2 * lanes + 1
    width = peers * lanes
    span = width // parts
    grad_filter_ref[...] = in_ref[pl.ds(2 * lanes, peers, stride=rows), :]
    copies = [pltpu.make_async_copy(grad_filter_ref, grad_filter_hbm, sems.at[4, 0])]
    copies[0].start()
    sides = (
        (
            (query_ref, output_ref, output_hbm),
            (grad_ref, grad_query_ref, grad_query_hbm),
        ),
        (
            (value_ref, grad_key_ref, grad_key_hbm),
            (key_ref, grad_value_ref, grad_value_hbm),
        ),
    )
    for index, pair in enumerate(sides):
        for part in range(parts):
            for start in range(part * span, (part + 1) * span, 128):
                columns = pl.ds(start, 128)
                blocks = []
                for offset in range(0, 128, lanes):
                    first = (start + offset) // lanes * rows + index * lanes
                    blocks.append(in_ref[pl.ds(first, lanes), :])
                signal = jnp.concatenate(blocks, axis=0).T
                for factor, target, _ in pair:
                    target[:, columns] = (factor[:, columns].astype(f32) * signal).astype(bf16)
            columns = pl.ds(part * span, span)
            for side, (_, source, target) in enumerate(pair):
                copy = pltpu.make_async_copy(
                    source.at[:, columns], target.at[:, columns], sems.at[2 * index + side, part]
                )
                copy.start()
                copies.append(copy)
    for copy in copies:
        copy.wait()


def exchange(signal):
    pieces = signal.reshape(signal.shape[0], 1, signal.shape[1])
    pieces = lax.all_to_all(pieces, "context", 0, 0, tiled=True)
    return pieces.reshape(signal.shape)


def solution(mesh):
    peers = mesh.shape["context"]
    params = pltpu.CompilerParams(vmem_limit_bytes=48 * 1024 * 1024)

    def local(query_gate, key_gate, value_in, filter_raw, grad_out):
        inner, width = query_gate.shape
        lanes = width // filter_raw.shape[1]
        rows = 2 * lanes + 1
        scale = 1.0 / math.sqrt(peers * inner)
        packed = jax.ShapeDtypeStruct((peers * rows, inner), f32)
        held_wide = pltpu.VMEM((inner, width), bf16)
        held_filter = pltpu.VMEM((peers, inner), f32)
        sent = pl.pallas_call(
            lambda *refs: pack_kernel(peers, lanes, 1, *refs),
            out_shape=packed,
            in_specs=[pl.BlockSpec(memory_space=pltpu.HBM)] * 5,
            scratch_shapes=[held_wide] * 4
            + [held_filter, pltpu.SemaphoreType.DMA((3, 2, 1))],
            compiler_params=params,
            name="pack",
        )(
            *(
                pltpu.with_memory_space_constraint(array, pltpu.HBM)
                for array in (query_gate, key_gate, value_in, filter_raw.T, grad_out)
            )
        )
        held = exchange(sent)
        result = pl.pallas_call(
            lambda *refs: convolve_kernel(peers, lanes, *refs),
            out_shape=packed,
            scratch_shapes=[pltpu.VMEM((peers * rows, 2 * inner), bf16)] * 2,
            compiler_params=params,
            name="convolve",
        )(held, *(jnp.asarray(table) for table in tables(peers, inner, scale)))
        back = exchange(result)
        wide = jax.ShapeDtypeStruct((inner, width), bf16)
        *outputs, grad_filter = pl.pallas_call(
            lambda *refs: unpack_kernel(peers, lanes, 2, *refs),
            out_shape=(wide,) * 4 + (jax.ShapeDtypeStruct((peers, inner), f32),),
            out_specs=(pl.BlockSpec(memory_space=pltpu.HBM),) * 5,
            scratch_shapes=[held_wide] * 4
            + [held_filter, pltpu.SemaphoreType.DMA((5, 2))],
            compiler_params=params,
            name="unpack",
        )(back, query_gate, key_gate, value_in, grad_out)
        return (*outputs, grad_filter.T)

    spec = P("context", "tensor")
    return jax.shard_map(
        local, mesh=mesh, in_specs=(spec,) * 5, out_specs=(spec,) * 5, check_vma=False
    )
```

```python
import math

import jax
import jax.numpy as jnp
import ml_dtypes
import numpy as np
from jax import lax
from jax.experimental import pallas as pl
from jax.experimental.pallas import tpu as pltpu
from jax.sharding import PartitionSpec as P

bf16 = jnp.bfloat16
f32 = jnp.float32


def split_table(table):
    high = table.astype(np.float32).astype(ml_dtypes.bfloat16)
    low = (table - high.astype(np.float64)).astype(np.float32).astype(ml_dtypes.bfloat16)
    return high, low


def tables(blocks, inner, scale):
    points = 2 * blocks * inner
    a = np.arange(blocks)
    b = np.arange(inner)
    odd = 2 * np.arange(blocks) + 1
    across = np.pi * np.outer(odd, a) / (2 * blocks)
    order = np.concatenate([np.arange(0, blocks, 2), np.arange(1, blocks, 2)])
    fore = np.concatenate([np.cos(across), -np.sin(across)], axis=0)[:, order]
    back = np.concatenate([np.cos(across), -np.sin(across)], axis=0).T
    fore_high, fore_low = split_table(fore)
    back_high, back_low = split_table(back)
    turn = np.pi * np.outer(odd, b) / points
    turn_fore = np.stack([np.cos(turn), -np.sin(turn)]).astype(np.float32)
    turn_back = (np.stack([np.cos(turn), np.sin(turn)]) * (2.0 * scale / points)).astype(np.float32)
    within = 2 * np.pi * np.outer(b, b) / inner
    cosine, sine = np.cos(within), np.sin(within)
    wide_fore = np.block([[cosine, -sine], [sine, cosine]])
    wide_back = np.block([[cosine, sine], [-sine, cosine]])
    fh, fl = split_table(wide_fore)
    bh, bl = split_table(wide_back)
    return (
        np.concatenate([fore_high, fore_high, fore_low], axis=1),
        np.concatenate([back_high, back_high, back_low], axis=1),
        np.concatenate([fh, fh, fl], axis=0),
        np.concatenate([bh, bh, bl], axis=0),
        turn_fore,
        turn_back,
    )


def halves(value):
    high = value.astype(bf16)
    return high, (value - high.astype(f32)).astype(bf16)


def dot(left, right):
    return jnp.dot(left, right, preferred_element_type=f32)


def pack_kernel(
    hosts,
    lanes,
    early,
    query_hbm,
    key_hbm,
    value_hbm,
    filter_hbm,
    grad_hbm,
    own_ref,
    other_ref,
    early_ref,
    query_ref,
    key_ref,
    value_ref,
    grad_ref,
    filter_ref,
    sems,
):
    rows = 2 * lanes + 1
    half = hosts * lanes
    arrays = (
        (key_hbm, key_ref),
        (value_hbm, value_ref),
        (grad_hbm, grad_ref),
        (query_hbm, query_ref),
        (filter_hbm, filter_ref),
    )
    copies = []
    for index, (source, target) in enumerate(arrays):
        copies.append(pltpu.make_async_copy(source, target, sems.at[index]))
        copies[-1].start()
    core = lax.rem(lax.axis_index("context"), 2)
    for index, (left, right) in enumerate(((key_ref, value_ref), (grad_ref, query_ref))):
        copies[2 * index].wait()
        copies[2 * index + 1].wait()
        for target, side in ((other_ref, 1 - core), (own_ref, core)):
            for start in range(0, half, 128):
                columns = pl.ds(pl.multiple_of(side * half + start, 128), 128)
                product = left[:, columns].astype(f32) * right[:, columns].astype(f32)
                turned = product.T
                for offset in range(0, 128, lanes):
                    host = (start + offset) // lanes
                    block = turned[offset : offset + lanes]
                    target[pl.ds(host * rows + index * lanes, lanes), :] = block
                    if target is own_ref and index == 0:
                        early_ref[pl.ds(host * early, early), :] = block[:early]
    copies[4].wait()
    for target, side in ((other_ref, 1 - core), (own_ref, core)):
        target[pl.ds(2 * lanes, hosts, stride=rows), :] = filter_ref[
            pl.ds(pl.multiple_of(side * hosts, hosts), hosts), :
        ]


def join_kernel(hosts, first_ref, second_ref, out_ref):
    rows = first_ref.shape[0] // hosts
    more = second_ref.shape[0] // hosts
    for host in range(hosts):
        start = host * (rows + more)
        out_ref[pl.ds(start, rows), :] = first_ref[pl.ds(host * rows, rows), :]
        out_ref[pl.ds(start + rows, more), :] = second_ref[pl.ds(host * more, more), :]


def join_late_kernel(hosts, early, own_ref, given_ref, out_ref):
    rows = own_ref.shape[0] // hosts
    late = rows - early
    for host in range(hosts):
        start = host * (rows + late)
        out_ref[pl.ds(start, late), :] = own_ref[pl.ds(host * rows + early, late), :]
        out_ref[pl.ds(start + late, rows), :] = given_ref[pl.ds(host * rows, rows), :]


def convolve_kernel(
    peers,
    lanes,
    early,
    in_refs,
    fore_ref,
    back_ref,
    wide_fore_ref,
    wide_back_ref,
    turn_fore_ref,
    turn_back_ref,
    out_ref,
    high_ref,
    low_ref,
):
    rows = 2 * lanes + 1
    inner = out_ref.shape[1]
    hosts = peers // 2
    chunk = 4

    def place(first, count=1):
        return pl.ds(first * peers, count * peers)

    def put(first, value):
        high, low = halves(value)
        here = pl.ds(first * peers, value.shape[0])
        high_ref[here, :] = high
        low_ref[here, :] = low

    def transformed(first, count, table_ref):
        high = high_ref[place(first, count), :]
        low = low_ref[place(first, count), :]
        return dot(jnp.concatenate([high, low, high], axis=1), table_ref[...])

    def rotated(real, imag, turn_ref):
        cosine, sine = turn_ref[0], turn_ref[1]
        return jnp.concatenate(
            [real * cosine - imag * sine, real * sine + imag * cosine], axis=1
        )

    def received(row):
        if len(in_refs) == 1:
            even = in_refs[0][pl.ds(row, hosts, stride=2 * rows), :]
            odd = in_refs[0][pl.ds(rows + row, hosts, stride=2 * rows), :]
        else:
            stride = 2 * rows - early
            even = in_refs[1][pl.ds(rows - early + row, hosts, stride=stride), :]
            if row < early:
                odd = in_refs[0][pl.ds(row, hosts, stride=early), :]
            else:
                odd = in_refs[1][pl.ds(row - early, hosts, stride=stride), :]
        return jnp.concatenate([even, odd], axis=0)

    fore = fore_ref[...]
    order = [2 * lanes] + list(range(2 * lanes))
    for start in range(0, rows, 2):
        chosen = order[start : start + 2]
        columns = []
        for row in chosen:
            high, low = halves(received(row))
            columns.append(jnp.concatenate([high, low, high], axis=0))
        spread = dot(fore, jnp.concatenate(columns, axis=1))
        for index, row in enumerate(chosen):
            part = spread[:, index * inner : (index + 1) * inner]
            put(row, rotated(part[:peers], part[peers:], turn_fore_ref))

    filt = transformed(2 * lanes, 1, wide_fore_ref)
    filt_re, filt_im = filt[:, :inner], filt[:, inner:]
    corr_re = jnp.zeros((peers, inner), f32)
    corr_im = jnp.zeros((peers, inner), f32)
    for first in range(0, lanes, chunk):
        gated = transformed(first, chunk, wide_fore_ref)
        grad = transformed(lanes + first, chunk, wide_fore_ref)
        for index in range(chunk):
            part = slice(index * peers, (index + 1) * peers)
            gated_re, gated_im = gated[part, :inner], gated[part, inner:]
            grad_re, grad_im = grad[part, :inner], grad[part, inner:]
            put(
                first + index,
                jnp.concatenate(
                    [
                        gated_re * filt_re - gated_im * filt_im,
                        gated_re * filt_im + gated_im * filt_re,
                    ],
                    axis=1,
                ),
            )
            put(
                lanes + first + index,
                jnp.concatenate(
                    [
                        filt_re * grad_re + filt_im * grad_im,
                        filt_re * grad_im - filt_im * grad_re,
                    ],
                    axis=1,
                ),
            )
            corr_re = corr_re + (gated_re * grad_re + gated_im * grad_im)
            corr_im = corr_im + (gated_re * grad_im - gated_im * grad_re)
    put(2 * lanes, jnp.concatenate([corr_re, corr_im], axis=1))

    for first in range(0, rows, chunk):
        count = min(chunk, rows - first)
        spec = transformed(first, count, wide_back_ref)
        for index in range(count):
            part = spec[index * peers : (index + 1) * peers]
            put(first + index, rotated(part[:, :inner], part[:, inner:], turn_back_ref))

    back = back_ref[...]
    for start in range(0, rows, 2):
        columns = []
        for row in range(start, min(start + 2, rows)):
            high, low = high_ref[place(row), :], low_ref[place(row), :]
            high = jnp.concatenate([high[:, :inner], high[:, inner:]], axis=0)
            low = jnp.concatenate([low[:, :inner], low[:, inner:]], axis=0)
            columns.append(jnp.concatenate([high, low, high], axis=0))
        signal = dot(back, jnp.concatenate(columns, axis=1))
        for index in range(len(columns)):
            out_ref[pl.ds(start + index, peers, stride=rows), :] = signal[
                :, index * inner : (index + 1) * inner
            ]


def unpack_kernel(
    hosts,
    lanes,
    own_ref,
    given_ref,
    query_ref,
    key_ref,
    value_ref,
    grad_ref,
    output_hbm,
    grad_query_hbm,
    grad_key_hbm,
    grad_value_hbm,
    grad_filter_hbm,
    output_ref,
    grad_query_ref,
    grad_key_ref,
    grad_value_ref,
    grad_filter_ref,
    sems,
):
    rows = 2 * lanes + 1
    half = hosts * lanes
    sides = (
        (
            (query_ref, output_ref, output_hbm),
            (grad_ref, grad_query_ref, grad_query_hbm),
        ),
        (
            (value_ref, grad_key_ref, grad_key_hbm),
            (key_ref, grad_value_ref, grad_value_hbm),
        ),
    )

    def finish(core):
        mine = core * rows
        copies = []
        for part, source in ((core, own_ref), (1 - core, given_ref)):
            grad_filter_ref[pl.ds(part * hosts, hosts), :] = source[
                pl.ds(mine + 2 * lanes, hosts, stride=2 * rows), :
            ]
        copies.append(pltpu.make_async_copy(grad_filter_ref, grad_filter_hbm, sems.at[4, 0]))
        copies[-1].start()
        for index, pair in enumerate(sides):
            for part, source in ((core, own_ref), (1 - core, given_ref)):
                for start in range(0, half, 128):
                    columns = pl.ds(part * half + start, 128)
                    blocks = []
                    for offset in range(0, 128, lanes):
                        host = (start + offset) // lanes
                        first = host * 2 * rows + mine + index * lanes
                        blocks.append(source[pl.ds(first, lanes), :])
                    signal = jnp.concatenate(blocks, axis=0).T
                    for factor, target, _ in pair:
                        target[:, columns] = (factor[:, columns].astype(f32) * signal).astype(
                            bf16
                        )
                columns = pl.ds(part * half, half)
                for side, (_, kept, target) in enumerate(pair):
                    copies.append(
                        pltpu.make_async_copy(
                            kept.at[:, columns],
                            target.at[:, columns],
                            sems.at[2 * index + side, part],
                        )
                    )
                    copies[-1].start()
        for copy in copies:
            copy.wait()

    core = lax.rem(lax.axis_index("context"), 2)

    @pl.when(core == 0)
    def _():
        finish(0)

    @pl.when(core == 1)
    def _():
        finish(1)


def exchange(signal, groups):
    pieces = signal.reshape(signal.shape[0], 1, signal.shape[1])
    pieces = lax.all_to_all(pieces, "context", 0, 0, axis_index_groups=groups, tiled=True)
    return pieces.reshape(signal.shape)


def solution(mesh):
    peers = mesh.shape["context"]
    hosts = peers // 2
    groups = [[2 * host + core for host in range(hosts)] for core in range(2)]
    swap = [(rank, rank ^ 1) for rank in range(peers)]
    params = pltpu.CompilerParams(vmem_limit_bytes=48 * 1024 * 1024)
    early = 8

    def local(query_gate, key_gate, value_in, filter_raw, grad_out):
        inner, width = query_gate.shape
        lanes = width // filter_raw.shape[1]
        rows = 2 * lanes + 1
        scale = 1.0 / math.sqrt(peers * inner)
        held_wide = pltpu.VMEM((inner, width), bf16)
        held_filter = pltpu.VMEM((peers, inner), f32)
        constants = [jnp.asarray(table) for table in tables(peers, inner, scale)]

        def block_rows(count):
            return jax.ShapeDtypeStruct((hosts * count, inner), f32)

        own, other, ahead = pl.pallas_call(
            lambda *refs: pack_kernel(hosts, lanes, early, *refs),
            out_shape=(block_rows(rows), block_rows(rows), block_rows(early)),
            in_specs=[pl.BlockSpec(memory_space=pltpu.HBM)] * 5,
            scratch_shapes=[held_wide] * 4 + [held_filter, pltpu.SemaphoreType.DMA((5,))],
            compiler_params=params,
            name="pack",
        )(
            *(
                pltpu.with_memory_space_constraint(array, pltpu.HBM)
                for array in (query_gate, key_gate, value_in, filter_raw.T, grad_out)
            )
        )

        def convolve(*held):
            count = len(held)
            return pl.pallas_call(
                lambda *refs: convolve_kernel(peers, lanes, early, refs[:count], *refs[count:]),
                out_shape=block_rows(2 * rows),
                scratch_shapes=[pltpu.VMEM((peers * rows, 2 * inner), bf16)] * 2,
                compiler_params=params,
                name="convolve",
            )(*held, *constants)

        def join(kernel, size, *parts):
            return pl.pallas_call(
                kernel, out_shape=block_rows(size), compiler_params=params, name="join"
            )(*parts)

        leads = lax.rem(lax.axis_index("context"), 2) == 0
        given = lax.ppermute(other, "context", swap)

        def lead(own, ahead, given):
            sent = join(lambda *refs: join_kernel(hosts, *refs), 2 * rows, own, given)
            return exchange(convolve(exchange(sent, groups)), groups)

        def follow(own, ahead, given):
            sent = join(
                lambda *refs: join_late_kernel(hosts, early, *refs), 2 * rows - early, own, given
            )
            held_ahead = exchange(ahead, groups)
            return exchange(convolve(held_ahead, exchange(sent, groups)), groups)

        back = lax.cond(leads, lead, follow, own, ahead, given)
        back_given = lax.ppermute(back, "context", swap)
        wide = jax.ShapeDtypeStruct((inner, width), bf16)
        *outputs, grad_filter = pl.pallas_call(
            lambda *refs: unpack_kernel(hosts, lanes, *refs),
            out_shape=(wide,) * 4 + (jax.ShapeDtypeStruct((peers, inner), f32),),
            out_specs=(pl.BlockSpec(memory_space=pltpu.HBM),) * 5,
            scratch_shapes=[held_wide] * 4 + [held_filter, pltpu.SemaphoreType.DMA((5, 2))],
            compiler_params=params,
            name="unpack",
        )(back, back_given, query_gate, key_gate, value_in, grad_out)
        return (*outputs, grad_filter.T)

    spec = P("context", "tensor")
    return jax.shard_map(
        local, mesh=mesh, in_specs=(spec,) * 5, out_specs=(spec,) * 5, check_vma=False
    )
```

```python
import math

import jax
import jax.numpy as jnp
import ml_dtypes
import numpy as np
from jax import lax
from jax.experimental import pallas as pl
from jax.experimental.pallas import tpu as pltpu
from jax.sharding import PartitionSpec as P

bf16 = jnp.bfloat16
f32 = jnp.float32


def split_table(table):
    high = table.astype(np.float32).astype(ml_dtypes.bfloat16)
    low = (table - high.astype(np.float64)).astype(np.float32).astype(ml_dtypes.bfloat16)
    return high, low


def tables(blocks, inner, scale):
    points = 2 * blocks * inner
    a = np.arange(blocks)
    b = np.arange(inner)
    odd = 2 * np.arange(blocks) + 1
    across = np.pi * np.outer(odd, a) / (2 * blocks)
    order = np.concatenate([np.arange(0, blocks, 2), np.arange(1, blocks, 2)])
    fore = np.concatenate([np.cos(across), -np.sin(across)], axis=0)[:, order]
    back = np.concatenate([np.cos(across), -np.sin(across)], axis=0).T
    fore_high, fore_low = split_table(fore)
    back_high, back_low = split_table(back)
    turn = np.pi * np.outer(odd, b) / points
    turn_fore = np.stack([np.cos(turn), -np.sin(turn)]).astype(np.float32)
    turn_back = (np.stack([np.cos(turn), np.sin(turn)]) * (2.0 * scale / points)).astype(np.float32)
    within = 2 * np.pi * np.outer(b, b) / inner
    cosine, sine = np.cos(within), np.sin(within)
    wide_fore = np.block([[cosine, -sine], [sine, cosine]])
    wide_back = np.block([[cosine, sine], [-sine, cosine]])
    fh, fl = split_table(wide_fore)
    bh, bl = split_table(wide_back)
    return (
        np.concatenate([fore_high, fore_high, fore_low], axis=1),
        np.concatenate([back_high, back_high, back_low], axis=1),
        np.concatenate([fh, fh, fl], axis=0),
        np.concatenate([bh, bh, bl], axis=0),
        turn_fore,
        turn_back,
    )


def halves(value):
    high = value.astype(bf16)
    return high, (value - high.astype(f32)).astype(bf16)


def dot(left, right):
    return jnp.dot(left, right, preferred_element_type=f32)


def pack_kernel(hosts, lanes, other, *refs):
    sources, out_ref, targets, sems = refs[:5], refs[5], refs[6:11], refs[11]
    rows = 2 * lanes + 1
    half = hosts * lanes
    core = lax.rem(lax.axis_index("context"), 2)
    part = 1 - core if other else core
    columns = pl.ds(pl.multiple_of(part * half, half), half)
    copies = []
    for index in range(4):
        source = sources[index].at[:, columns]
        copies.append(pltpu.make_async_copy(source, targets[index], sems.at[index]))
    source = sources[4].at[pl.ds(pl.multiple_of(part * hosts, hosts), hosts), :]
    copies.append(pltpu.make_async_copy(source, targets[4], sems.at[4]))
    for copy in copies:
        copy.start()
    for index in range(2):
        copies[2 * index].wait()
        copies[2 * index + 1].wait()
        left, right = targets[2 * index], targets[2 * index + 1]
        for start in range(0, half, 128):
            place = pl.ds(start, 128)
            product = left[:, place].astype(f32) * right[:, place].astype(f32)
            turned = product.T
            for offset in range(0, 128, lanes):
                first = (start + offset) // lanes * rows + index * lanes
                out_ref[pl.ds(first, lanes), :] = turned[offset : offset + lanes]
    copies[4].wait()
    out_ref[pl.ds(2 * lanes, hosts, stride=rows), :] = targets[4][...]


def take_kernel(hosts, first, own_ref, out_ref):
    rows = own_ref.shape[0] // hosts
    count = out_ref.shape[0] // hosts
    for host in range(hosts):
        out_ref[pl.ds(host * count, count), :] = own_ref[pl.ds(host * rows + first, count), :]


def take_other_kernel(hosts, back_ref, out_ref):
    core = lax.rem(lax.axis_index("context"), 2)

    @pl.when(core == 0)
    def _():
        take_kernel(hosts, out_ref.shape[0] // hosts, back_ref, out_ref)

    @pl.when(core == 1)
    def _():
        take_kernel(hosts, 0, back_ref, out_ref)


def join_kernel(hosts, first_ref, second_ref, out_ref):
    rows = first_ref.shape[0] // hosts
    more = second_ref.shape[0] // hosts
    for host in range(hosts):
        start = host * (rows + more)
        out_ref[pl.ds(start, rows), :] = first_ref[pl.ds(host * rows, rows), :]
        out_ref[pl.ds(start + rows, more), :] = second_ref[pl.ds(host * more, more), :]


def join_late_kernel(hosts, early, own_ref, given_ref, out_ref):
    rows = own_ref.shape[0] // hosts
    late = rows - early
    for host in range(hosts):
        start = host * (rows + late)
        out_ref[pl.ds(start, late), :] = own_ref[pl.ds(host * rows + early, late), :]
        out_ref[pl.ds(start + late, rows), :] = given_ref[pl.ds(host * rows, rows), :]


def convolve_kernel(
    peers,
    lanes,
    early,
    in_refs,
    fore_ref,
    back_ref,
    wide_fore_ref,
    wide_back_ref,
    turn_fore_ref,
    turn_back_ref,
    out_ref,
    high_ref,
    low_ref,
):
    rows = 2 * lanes + 1
    inner = out_ref.shape[1]
    hosts = peers // 2
    chunk = 4

    def place(first, count=1):
        return pl.ds(first * peers, count * peers)

    def put(first, value):
        high, low = halves(value)
        here = pl.ds(first * peers, value.shape[0])
        high_ref[here, :] = high
        low_ref[here, :] = low

    def transformed(first, count, table_ref):
        high = high_ref[place(first, count), :]
        low = low_ref[place(first, count), :]
        return dot(jnp.concatenate([high, low, high], axis=1), table_ref[...])

    def rotated(real, imag, turn_ref):
        cosine, sine = turn_ref[0], turn_ref[1]
        return jnp.concatenate(
            [real * cosine - imag * sine, real * sine + imag * cosine], axis=1
        )

    def received(row):
        if len(in_refs) == 1:
            even = in_refs[0][pl.ds(row, hosts, stride=2 * rows), :]
            odd = in_refs[0][pl.ds(rows + row, hosts, stride=2 * rows), :]
        else:
            stride = 2 * rows - early
            even = in_refs[1][pl.ds(rows - early + row, hosts, stride=stride), :]
            if row < early:
                odd = in_refs[0][pl.ds(row, hosts, stride=early), :]
            else:
                odd = in_refs[1][pl.ds(row - early, hosts, stride=stride), :]
        return jnp.concatenate([even, odd], axis=0)

    fore = fore_ref[...]
    order = [2 * lanes] + list(range(2 * lanes))
    for start in range(0, rows, 2):
        chosen = order[start : start + 2]
        columns = []
        for row in chosen:
            high, low = halves(received(row))
            columns.append(jnp.concatenate([high, low, high], axis=0))
        spread = dot(fore, jnp.concatenate(columns, axis=1))
        for index, row in enumerate(chosen):
            part = spread[:, index * inner : (index + 1) * inner]
            put(row, rotated(part[:peers], part[peers:], turn_fore_ref))

    filt = transformed(2 * lanes, 1, wide_fore_ref)
    filt_re, filt_im = filt[:, :inner], filt[:, inner:]
    corr_re = jnp.zeros((peers, inner), f32)
    corr_im = jnp.zeros((peers, inner), f32)
    for first in range(0, lanes, chunk):
        gated = transformed(first, chunk, wide_fore_ref)
        grad = transformed(lanes + first, chunk, wide_fore_ref)
        for index in range(chunk):
            part = slice(index * peers, (index + 1) * peers)
            gated_re, gated_im = gated[part, :inner], gated[part, inner:]
            grad_re, grad_im = grad[part, :inner], grad[part, inner:]
            put(
                first + index,
                jnp.concatenate(
                    [
                        gated_re * filt_re - gated_im * filt_im,
                        gated_re * filt_im + gated_im * filt_re,
                    ],
                    axis=1,
                ),
            )
            put(
                lanes + first + index,
                jnp.concatenate(
                    [
                        filt_re * grad_re + filt_im * grad_im,
                        filt_re * grad_im - filt_im * grad_re,
                    ],
                    axis=1,
                ),
            )
            corr_re = corr_re + (gated_re * grad_re + gated_im * grad_im)
            corr_im = corr_im + (gated_re * grad_im - gated_im * grad_re)
    put(2 * lanes, jnp.concatenate([corr_re, corr_im], axis=1))

    for first in range(0, rows, chunk):
        count = min(chunk, rows - first)
        spec = transformed(first, count, wide_back_ref)
        for index in range(count):
            part = spec[index * peers : (index + 1) * peers]
            put(first + index, rotated(part[:, :inner], part[:, inner:], turn_back_ref))

    back = back_ref[...]
    for start in range(0, rows, 2):
        columns = []
        for row in range(start, min(start + 2, rows)):
            high, low = high_ref[place(row), :], low_ref[place(row), :]
            high = jnp.concatenate([high[:, :inner], high[:, inner:]], axis=0)
            low = jnp.concatenate([low[:, :inner], low[:, inner:]], axis=0)
            columns.append(jnp.concatenate([high, low, high], axis=0))
        signal = dot(back, jnp.concatenate(columns, axis=1))
        for index in range(len(columns)):
            out_ref[pl.ds(start + index, peers, stride=rows), :] = signal[
                :, index * inner : (index + 1) * inner
            ]


def unpack_kernel(hosts, lanes, given, *refs):
    if given:
        in_ref, *refs = refs
        refs = refs[:4] + refs[9:]
    else:
        in_ref, *refs = refs
    query_ref, key_ref, value_ref, grad_ref, *refs = refs
    targets, kept, filter_ref, sems = refs[:5], refs[5:9], refs[9], refs[10]
    rows = 2 * lanes + 1
    half = hosts * lanes
    pairs = ((query_ref, grad_ref), (value_ref, key_ref))
    core = lax.rem(lax.axis_index("context"), 2)
    part = 1 - core if given else core
    place = pl.ds(pl.multiple_of(part * half, half), half)

    def finish(first, stride):
        filter_ref[...] = in_ref[pl.ds(first + 2 * lanes, hosts, stride=stride), :]
        copies = [
            pltpu.make_async_copy(
                filter_ref,
                targets[4].at[pl.ds(pl.multiple_of(part * hosts, hosts), hosts), :],
                sems.at[4],
            )
        ]
        copies[0].start()
        for index, pair in enumerate(pairs):
            for start in range(0, half, 128):
                blocks = []
                for offset in range(0, 128, lanes):
                    row = (start + offset) // lanes * stride + first + index * lanes
                    blocks.append(in_ref[pl.ds(row, lanes), :])
                signal = jnp.concatenate(blocks, axis=0).T
                columns = pl.ds(pl.multiple_of(part * half + start, 128), 128)
                for side, factor in enumerate(pair):
                    kept[2 * index + side][:, pl.ds(start, 128)] = (
                        factor[:, columns].astype(f32) * signal
                    ).astype(bf16)
            for side in range(2):
                number = 2 * index + side
                copies.append(
                    pltpu.make_async_copy(
                        kept[number], targets[number].at[:, place], sems.at[number]
                    )
                )
                copies[-1].start()
        for copy in copies:
            copy.wait()

    if given:
        finish(0, rows)
        return

    @pl.when(core == 0)
    def _():
        finish(0, 2 * rows)

    @pl.when(core == 1)
    def _():
        finish(rows, 2 * rows)


def exchange(signal, groups):
    pieces = signal.reshape(signal.shape[0], 1, signal.shape[1])
    pieces = lax.all_to_all(pieces, "context", 0, 0, axis_index_groups=groups, tiled=True)
    return pieces.reshape(signal.shape)


def solution(mesh):
    peers = mesh.shape["context"]
    hosts = peers // 2
    groups = [[2 * host + core for host in range(hosts)] for core in range(2)]
    swap = [(rank, rank ^ 1) for rank in range(peers)]
    params = pltpu.CompilerParams(vmem_limit_bytes=48 * 1024 * 1024)
    early = 4

    def local(query_gate, key_gate, value_in, filter_raw, grad_out):
        inner, width = query_gate.shape
        lanes = width // filter_raw.shape[1]
        rows = 2 * lanes + 1
        scale = 1.0 / math.sqrt(peers * inner)
        constants = [jnp.asarray(table) for table in tables(peers, inner, scale)]

        def block_rows(count):
            return jax.ShapeDtypeStruct((hosts * count, inner), f32)

        held_half = pltpu.VMEM((inner, width // 2), bf16)
        half_scratch = [held_half] * 4 + [
            pltpu.VMEM((hosts, inner), f32),
            pltpu.SemaphoreType.DMA((5,)),
        ]
        sources = [
            pltpu.with_memory_space_constraint(array, pltpu.HBM)
            for array in (key_gate, value_in, grad_out, query_gate, filter_raw.T)
        ]

        def pack(other):
            return pl.pallas_call(
                lambda *refs: pack_kernel(hosts, lanes, other, *refs),
                out_shape=block_rows(rows),
                in_specs=[pl.BlockSpec(memory_space=pltpu.HBM)] * 5,
                scratch_shapes=half_scratch,
                compiler_params=params,
                name="pack",
            )(*sources)

        given = lax.ppermute(pack(True), "context", swap)
        own = pack(False)

        def convolve(*held):
            count = len(held)
            return pl.pallas_call(
                lambda *refs: convolve_kernel(peers, lanes, early, refs[:count], *refs[count:]),
                out_shape=block_rows(2 * rows),
                scratch_shapes=[pltpu.VMEM((peers * rows, 2 * inner), bf16)] * 2,
                compiler_params=params,
                name="convolve",
            )(*held, *constants)

        def join(kernel, size, *parts):
            return pl.pallas_call(
                kernel, out_shape=block_rows(size), compiler_params=params, name="join"
            )(*parts)

        leads = lax.rem(lax.axis_index("context"), 2) == 0
        def lead(own, given):
            sent = join(lambda *refs: join_kernel(hosts, *refs), 2 * rows, own, given)
            return exchange(convolve(exchange(sent, groups)), groups)

        def follow(own, given):
            ahead = join(lambda *refs: take_kernel(hosts, 0, *refs), early, own)
            sent = join(
                lambda *refs: join_late_kernel(hosts, early, *refs), 2 * rows - early, own, given
            )
            held_ahead = exchange(ahead, groups)
            return exchange(convolve(held_ahead, exchange(sent, groups)), groups)

        back = lax.cond(leads, lead, follow, own, given)
        other_back = join(lambda *refs: take_other_kernel(hosts, *refs), rows, back)
        back_given = lax.ppermute(other_back, "context", swap)
        factors = (query_gate, key_gate, value_in, grad_out)
        wide = jax.ShapeDtypeStruct((inner, width), bf16)
        shapes = (wide,) * 4 + (jax.ShapeDtypeStruct((peers, inner), f32),)
        hbm = pl.BlockSpec(memory_space=pltpu.HBM)
        vmem = pl.BlockSpec(memory_space=pltpu.VMEM)

        def unpack(given, signal, *partial):
            return pl.pallas_call(
                lambda *refs: unpack_kernel(hosts, lanes, given, *refs),
                out_shape=shapes,
                in_specs=[vmem] * 5 + [hbm] * len(partial),
                out_specs=(hbm,) * 5,
                scratch_shapes=half_scratch,
                input_output_aliases={5 + index: index for index in range(len(partial))},
                compiler_params=params,
                name="unpack",
            )(signal, *factors, *partial)

        *outputs, grad_filter = unpack(True, back_given, *unpack(False, back))
        return (*outputs, grad_filter.T)

    spec = P("context", "tensor")
    return jax.shard_map(
        local, mesh=mesh, in_specs=(spec,) * 5, out_specs=(spec,) * 5, check_vma=False
    )
```

```python
import math

import jax
import jax.numpy as jnp
import ml_dtypes
import numpy as np
from jax import lax
from jax.experimental import pallas as pl
from jax.experimental.pallas import tpu as pltpu
from jax.sharding import PartitionSpec as P

bf16 = jnp.bfloat16
f32 = jnp.float32


def split_table(table):
    high = table.astype(np.float32).astype(ml_dtypes.bfloat16)
    low = (table - high.astype(np.float64)).astype(np.float32).astype(ml_dtypes.bfloat16)
    return high, low


def tables(blocks, inner, scale):
    points = 2 * blocks * inner
    a = np.arange(blocks)
    b = np.arange(inner)
    odd = 2 * np.arange(blocks) + 1
    across = np.pi * np.outer(odd, a) / (2 * blocks)
    order = np.concatenate([np.arange(0, blocks, 2), np.arange(1, blocks, 2)])
    fore = np.concatenate([np.cos(across), -np.sin(across)], axis=0)[:, order]
    back = np.concatenate([np.cos(across), -np.sin(across)], axis=0).T
    fore_high, fore_low = split_table(fore)
    back_high, back_low = split_table(back)
    turn = np.pi * np.outer(odd, b) / points
    turn_fore = np.stack([np.cos(turn), -np.sin(turn)]).astype(np.float32)
    turn_back = (np.stack([np.cos(turn), np.sin(turn)]) * (2.0 * scale / points)).astype(np.float32)
    within = 2 * np.pi * np.outer(b, b) / inner
    cosine, sine = np.cos(within), np.sin(within)
    wide_fore = np.block([[cosine, -sine], [sine, cosine]])
    wide_back = np.block([[cosine, sine], [-sine, cosine]])
    fh, fl = split_table(wide_fore)
    bh, bl = split_table(wide_back)
    return (
        np.concatenate([fore_high, fore_high, fore_low], axis=1),
        np.block([[back_high, back_high], [back_low, np.zeros_like(back_low)]]),
        np.concatenate([fh, fh, fl], axis=0),
        np.concatenate([bh, bh, bl], axis=0),
        turn_fore,
        turn_back,
    )


def halves(value):
    high = value.astype(bf16)
    return high, (value - high.astype(f32)).astype(bf16)


def dot(left, right):
    return jnp.dot(left, right, preferred_element_type=f32)


def pack_kernel(hosts, lanes, other, *refs):
    sources, out_ref, targets, sems = refs[:5], refs[5], refs[6:11], refs[11]
    rows = 2 * lanes + 1
    half = hosts * lanes
    core = lax.rem(lax.axis_index("context"), 2)
    part = 1 - core if other else core
    columns = pl.ds(pl.multiple_of(part * half, half), half)
    copies = []
    for index in range(4):
        source = sources[index].at[:, columns]
        copies.append(pltpu.make_async_copy(source, targets[index], sems.at[index]))
    source = sources[4].at[pl.ds(pl.multiple_of(part * hosts, hosts), hosts), :]
    copies.append(pltpu.make_async_copy(source, targets[4], sems.at[4]))
    for copy in copies:
        copy.start()
    for index in range(2):
        copies[2 * index].wait()
        copies[2 * index + 1].wait()
        left, right = targets[2 * index], targets[2 * index + 1]
        for start in range(0, half, 128):
            place = pl.ds(start, 128)
            product = left[:, place].astype(f32) * right[:, place].astype(f32)
            turned = product.T
            for offset in range(0, 128, lanes):
                first = (start + offset) // lanes * rows + index * lanes
                out_ref[pl.ds(first, lanes), :] = turned[offset : offset + lanes]
    copies[4].wait()
    out_ref[pl.ds(2 * lanes, hosts, stride=rows), :] = targets[4][...]


def take_kernel(hosts, first, own_ref, out_ref):
    rows = own_ref.shape[0] // hosts
    count = out_ref.shape[0] // hosts
    for host in range(hosts):
        out_ref[pl.ds(host * count, count), :] = own_ref[pl.ds(host * rows + first, count), :]


def take_other_kernel(hosts, back_ref, out_ref):
    core = lax.rem(lax.axis_index("context"), 2)

    @pl.when(core == 0)
    def _():
        take_kernel(hosts, out_ref.shape[0] // hosts, back_ref, out_ref)

    @pl.when(core == 1)
    def _():
        take_kernel(hosts, 0, back_ref, out_ref)


def join_kernel(hosts, first_ref, second_ref, out_ref):
    rows = first_ref.shape[0] // hosts
    more = second_ref.shape[0] // hosts
    for host in range(hosts):
        start = host * (rows + more)
        out_ref[pl.ds(start, rows), :] = first_ref[pl.ds(host * rows, rows), :]
        out_ref[pl.ds(start + rows, more), :] = second_ref[pl.ds(host * more, more), :]


def join_late_kernel(hosts, early, own_ref, given_ref, out_ref):
    rows = own_ref.shape[0] // hosts
    late = rows - early
    for host in range(hosts):
        start = host * (rows + late)
        out_ref[pl.ds(start, late), :] = own_ref[pl.ds(host * rows + early, late), :]
        out_ref[pl.ds(start + late, rows), :] = given_ref[pl.ds(host * rows, rows), :]


def convolve_kernel(
    peers,
    lanes,
    early,
    in_refs,
    fore_ref,
    back_ref,
    wide_fore_ref,
    wide_back_ref,
    turn_fore_ref,
    turn_back_ref,
    out_ref,
    high_ref,
    low_ref,
):
    rows = 2 * lanes + 1
    inner = out_ref.shape[1]
    hosts = peers // 2
    chunk = 4

    def place(first, count=1):
        return pl.ds(first * peers, count * peers)

    def put(first, value):
        high, low = halves(value)
        here = pl.ds(first * peers, value.shape[0])
        high_ref[here, :] = high
        low_ref[here, :] = low

    def transformed(first, count, table_ref):
        high = high_ref[place(first, count), :]
        low = low_ref[place(first, count), :]
        return dot(jnp.concatenate([high, low, high], axis=1), table_ref[...])

    def rotated(real, imag, turn_ref):
        cosine, sine = turn_ref[0], turn_ref[1]
        return jnp.concatenate(
            [real * cosine - imag * sine, real * sine + imag * cosine], axis=1
        )

    def received(row):
        if len(in_refs) == 1:
            even = in_refs[0][pl.ds(row, hosts, stride=2 * rows), :]
            odd = in_refs[0][pl.ds(rows + row, hosts, stride=2 * rows), :]
        else:
            stride = 2 * rows - early
            even = in_refs[1][pl.ds(rows - early + row, hosts, stride=stride), :]
            if row < early:
                odd = in_refs[0][pl.ds(row, hosts, stride=early), :]
            else:
                odd = in_refs[1][pl.ds(row - early, hosts, stride=stride), :]
        return jnp.concatenate([even, odd], axis=0)

    fore = fore_ref[...]
    order = [2 * lanes] + list(range(2 * lanes))
    for start in range(0, rows, 2):
        chosen = order[start : start + 2]
        columns = []
        for row in chosen:
            high, low = halves(received(row))
            columns.append(jnp.concatenate([high, low, high], axis=0))
        spread = dot(fore, jnp.concatenate(columns, axis=1))
        for index, row in enumerate(chosen):
            part = spread[:, index * inner : (index + 1) * inner]
            put(row, rotated(part[:peers], part[peers:], turn_fore_ref))

    filt = transformed(2 * lanes, 1, wide_fore_ref)
    filt_re, filt_im = filt[:, :inner], filt[:, inner:]
    corr_re = jnp.zeros((peers, inner), f32)
    corr_im = jnp.zeros((peers, inner), f32)
    for first in range(0, lanes, chunk):
        gated = transformed(first, chunk, wide_fore_ref)
        grad = transformed(lanes + first, chunk, wide_fore_ref)
        for index in range(chunk):
            part = slice(index * peers, (index + 1) * peers)
            gated_re, gated_im = gated[part, :inner], gated[part, inner:]
            grad_re, grad_im = grad[part, :inner], grad[part, inner:]
            put(
                first + index,
                jnp.concatenate(
                    [
                        gated_re * filt_re - gated_im * filt_im,
                        gated_re * filt_im + gated_im * filt_re,
                    ],
                    axis=1,
                ),
            )
            put(
                lanes + first + index,
                jnp.concatenate(
                    [
                        filt_re * grad_re + filt_im * grad_im,
                        filt_re * grad_im - filt_im * grad_re,
                    ],
                    axis=1,
                ),
            )
            corr_re = corr_re + (gated_re * grad_re + gated_im * grad_im)
            corr_im = corr_im + (gated_re * grad_im - gated_im * grad_re)
    put(2 * lanes, jnp.concatenate([corr_re, corr_im], axis=1))

    for first in range(0, rows, chunk):
        count = min(chunk, rows - first)
        spec = transformed(first, count, wide_back_ref)
        for index in range(count):
            part = spec[index * peers : (index + 1) * peers]
            put(first + index, rotated(part[:, :inner], part[:, inner:], turn_back_ref))

    back = back_ref[...]
    for start in range(0, rows, 2):
        columns = []
        for row in range(start, min(start + 2, rows)):
            high, low = high_ref[place(row), :], low_ref[place(row), :]
            high = jnp.concatenate([high[:, :inner], high[:, inner:]], axis=0)
            low = jnp.concatenate([low[:, :inner], low[:, inner:]], axis=0)
            columns.append(jnp.concatenate([high, low], axis=0))
        signal = dot(back, jnp.concatenate(columns, axis=1))
        signal = signal[:peers] + signal[peers:]
        for index in range(len(columns)):
            out_ref[pl.ds(start + index, peers, stride=rows), :] = signal[
                :, index * inner : (index + 1) * inner
            ]


def unpack_kernel(hosts, lanes, given, *refs):
    if given:
        in_ref, *refs = refs
        refs = refs[:4] + refs[9:]
    else:
        in_ref, *refs = refs
    query_ref, key_ref, value_ref, grad_ref, *refs = refs
    targets, kept, filter_ref, sems = refs[:5], refs[5:9], refs[9], refs[10]
    rows = 2 * lanes + 1
    half = hosts * lanes
    pairs = ((query_ref, grad_ref), (value_ref, key_ref))
    core = lax.rem(lax.axis_index("context"), 2)
    part = 1 - core if given else core
    place = pl.ds(pl.multiple_of(part * half, half), half)

    def finish(first, stride):
        filter_ref[...] = in_ref[pl.ds(first + 2 * lanes, hosts, stride=stride), :]
        copies = [
            pltpu.make_async_copy(
                filter_ref,
                targets[4].at[pl.ds(pl.multiple_of(part * hosts, hosts), hosts), :],
                sems.at[4],
            )
        ]
        copies[0].start()
        for index, pair in enumerate(pairs):
            for start in range(0, half, 128):
                blocks = []
                for offset in range(0, 128, lanes):
                    row = (start + offset) // lanes * stride + first + index * lanes
                    blocks.append(in_ref[pl.ds(row, lanes), :])
                signal = jnp.concatenate(blocks, axis=0).T
                columns = pl.ds(pl.multiple_of(part * half + start, 128), 128)
                for side, factor in enumerate(pair):
                    kept[2 * index + side][:, pl.ds(start, 128)] = (
                        factor[:, columns].astype(f32) * signal
                    ).astype(bf16)
            for side in range(2):
                number = 2 * index + side
                copies.append(
                    pltpu.make_async_copy(
                        kept[number], targets[number].at[:, place], sems.at[number]
                    )
                )
                copies[-1].start()
        for copy in copies:
            copy.wait()

    if given:
        finish(0, rows)
        return

    @pl.when(core == 0)
    def _():
        finish(0, 2 * rows)

    @pl.when(core == 1)
    def _():
        finish(rows, 2 * rows)


def exchange(signal, groups):
    pieces = signal.reshape(signal.shape[0], 1, signal.shape[1])
    pieces = lax.all_to_all(pieces, "context", 0, 0, axis_index_groups=groups, tiled=True)
    return pieces.reshape(signal.shape)


def solution(mesh):
    peers = mesh.shape["context"]
    hosts = peers // 2
    groups = [[2 * host + core for host in range(hosts)] for core in range(2)]
    swap = [(rank, rank ^ 1) for rank in range(peers)]
    params = pltpu.CompilerParams(vmem_limit_bytes=48 * 1024 * 1024)
    early = 3

    def local(query_gate, key_gate, value_in, filter_raw, grad_out):
        inner, width = query_gate.shape
        lanes = width // filter_raw.shape[1]
        rows = 2 * lanes + 1
        scale = 1.0 / math.sqrt(peers * inner)
        constants = [jnp.asarray(table) for table in tables(peers, inner, scale)]

        def block_rows(count):
            return jax.ShapeDtypeStruct((hosts * count, inner), f32)

        held_half = pltpu.VMEM((inner, width // 2), bf16)
        half_scratch = [held_half] * 4 + [
            pltpu.VMEM((hosts, inner), f32),
            pltpu.SemaphoreType.DMA((5,)),
        ]
        sources = [
            pltpu.with_memory_space_constraint(array, pltpu.HBM)
            for array in (key_gate, value_in, grad_out, query_gate, filter_raw.T)
        ]

        def pack(other):
            return pl.pallas_call(
                lambda *refs: pack_kernel(hosts, lanes, other, *refs),
                out_shape=block_rows(rows),
                in_specs=[pl.BlockSpec(memory_space=pltpu.HBM)] * 5,
                scratch_shapes=half_scratch,
                compiler_params=params,
                name="pack",
            )(*sources)

        given = lax.ppermute(pack(True), "context", swap)
        own = pack(False)

        def convolve(*held):
            count = len(held)
            return pl.pallas_call(
                lambda *refs: convolve_kernel(peers, lanes, early, refs[:count], *refs[count:]),
                out_shape=block_rows(2 * rows),
                scratch_shapes=[pltpu.VMEM((peers * rows, 2 * inner), bf16)] * 2,
                compiler_params=params,
                name="convolve",
            )(*held, *constants)

        def join(kernel, size, *parts):
            return pl.pallas_call(
                kernel, out_shape=block_rows(size), compiler_params=params, name="join"
            )(*parts)

        leads = lax.rem(lax.axis_index("context"), 2) == 0
        def lead(own, given):
            sent = join(lambda *refs: join_kernel(hosts, *refs), 2 * rows, own, given)
            return exchange(convolve(exchange(sent, groups)), groups)

        def follow(own, given):
            ahead = join(lambda *refs: take_kernel(hosts, 0, *refs), early, own)
            sent = join(
                lambda *refs: join_late_kernel(hosts, early, *refs), 2 * rows - early, own, given
            )
            held_ahead = exchange(ahead, groups)
            return exchange(convolve(held_ahead, exchange(sent, groups)), groups)

        back = lax.cond(leads, lead, follow, own, given)
        other_back = join(lambda *refs: take_other_kernel(hosts, *refs), rows, back)
        back_given = lax.ppermute(other_back, "context", swap)
        factors = (query_gate, key_gate, value_in, grad_out)
        wide = jax.ShapeDtypeStruct((inner, width), bf16)
        shapes = (wide,) * 4 + (jax.ShapeDtypeStruct((peers, inner), f32),)
        hbm = pl.BlockSpec(memory_space=pltpu.HBM)
        vmem = pl.BlockSpec(memory_space=pltpu.VMEM)

        def unpack(given, signal, *partial):
            return pl.pallas_call(
                lambda *refs: unpack_kernel(hosts, lanes, given, *refs),
                out_shape=shapes,
                in_specs=[vmem] * 5 + [hbm] * len(partial),
                out_specs=(hbm,) * 5,
                scratch_shapes=half_scratch,
                input_output_aliases={5 + index: index for index in range(len(partial))},
                compiler_params=params,
                name="unpack",
            )(signal, *factors, *partial)

        *outputs, grad_filter = unpack(True, back_given, *unpack(False, back))
        return (*outputs, grad_filter.T)

    spec = P("context", "tensor")
    return jax.shard_map(
        local, mesh=mesh, in_specs=(spec,) * 5, out_specs=(spec,) * 5, check_vma=False
    )
```

```python
import math

import jax
import jax.numpy as jnp
import ml_dtypes
import numpy as np
from jax import lax
from jax.experimental import pallas as pl
from jax.experimental.pallas import tpu as pltpu
from jax.sharding import PartitionSpec as P

bf16 = jnp.bfloat16
f32 = jnp.float32


def split_table(table):
    high = table.astype(np.float32).astype(ml_dtypes.bfloat16)
    low = (table - high.astype(np.float64)).astype(np.float32).astype(ml_dtypes.bfloat16)
    return high, low


def tables(blocks, inner, scale):
    points = 2 * blocks * inner
    a = np.arange(blocks)
    b = np.arange(inner)
    odd = 2 * np.arange(blocks) + 1
    across = np.pi * np.outer(odd, a) / (2 * blocks)
    order = np.concatenate([np.arange(0, blocks, 2), np.arange(1, blocks, 2)])
    fore = np.concatenate([np.cos(across), -np.sin(across)], axis=0)[:, order]
    back = np.concatenate([np.cos(across), -np.sin(across)], axis=0).T
    fore_high, fore_low = split_table(fore)
    back_high, back_low = split_table(back)
    turn = np.pi * np.outer(odd, b) / points
    turn_fore = np.stack([np.cos(turn), -np.sin(turn)]).astype(np.float32)
    turn_back = (np.stack([np.cos(turn), np.sin(turn)]) * (2.0 * scale / points)).astype(np.float32)
    within = 2 * np.pi * np.outer(b, b) / inner
    cosine, sine = np.cos(within), np.sin(within)
    wide_fore = np.block([[cosine, -sine], [sine, cosine]])
    wide_back = np.block([[cosine, sine], [-sine, cosine]])
    fh, fl = split_table(wide_fore)
    bh, bl = split_table(wide_back)
    return (
        np.concatenate([fore_high, fore_high, fore_low], axis=1),
        np.block([[back_high, back_high], [back_low, np.zeros_like(back_low)]]),
        np.concatenate([fh, fl], axis=0),
        np.concatenate([bh, bl], axis=0),
        turn_fore,
        turn_back,
    )


def halves(value):
    high = value.astype(bf16)
    return high, (value - high.astype(f32)).astype(bf16)


def dot(left, right):
    return jnp.dot(left, right, preferred_element_type=f32)


def pack_kernel(hosts, lanes, other, *refs):
    sources, out_ref, targets, sems = refs[:5], refs[5], refs[6:11], refs[11]
    rows = 2 * lanes + 1
    half = hosts * lanes
    core = lax.rem(lax.axis_index("context"), 2)
    part = 1 - core if other else core
    columns = pl.ds(pl.multiple_of(part * half, half), half)
    copies = []
    for index in range(4):
        source = sources[index].at[:, columns]
        copies.append(pltpu.make_async_copy(source, targets[index], sems.at[index]))
    source = sources[4].at[pl.ds(pl.multiple_of(part * hosts, hosts), hosts), :]
    copies.append(pltpu.make_async_copy(source, targets[4], sems.at[4]))
    for copy in copies:
        copy.start()
    for index in range(2):
        copies[2 * index].wait()
        copies[2 * index + 1].wait()
        left, right = targets[2 * index], targets[2 * index + 1]
        for start in range(0, half, 128):
            place = pl.ds(start, 128)
            product = left[:, place].astype(f32) * right[:, place].astype(f32)
            turned = product.T
            for offset in range(0, 128, lanes):
                first = (start + offset) // lanes * rows + index * lanes
                out_ref[pl.ds(first, lanes), :] = turned[offset : offset + lanes]
    copies[4].wait()
    out_ref[pl.ds(2 * lanes, hosts, stride=rows), :] = targets[4][...]


def take_kernel(hosts, first, own_ref, out_ref):
    rows = own_ref.shape[0] // hosts
    count = out_ref.shape[0] // hosts
    for host in range(hosts):
        out_ref[pl.ds(host * count, count), :] = own_ref[pl.ds(host * rows + first, count), :]


def take_other_kernel(hosts, back_ref, out_ref):
    core = lax.rem(lax.axis_index("context"), 2)

    @pl.when(core == 0)
    def _():
        take_kernel(hosts, out_ref.shape[0] // hosts, back_ref, out_ref)

    @pl.when(core == 1)
    def _():
        take_kernel(hosts, 0, back_ref, out_ref)


def join_kernel(hosts, first_ref, second_ref, out_ref):
    rows = first_ref.shape[0] // hosts
    more = second_ref.shape[0] // hosts
    for host in range(hosts):
        start = host * (rows + more)
        out_ref[pl.ds(start, rows), :] = first_ref[pl.ds(host * rows, rows), :]
        out_ref[pl.ds(start + rows, more), :] = second_ref[pl.ds(host * more, more), :]


def join_late_kernel(hosts, early, own_ref, given_ref, out_ref):
    rows = own_ref.shape[0] // hosts
    late = rows - early
    for host in range(hosts):
        start = host * (rows + late)
        out_ref[pl.ds(start, late), :] = own_ref[pl.ds(host * rows + early, late), :]
        out_ref[pl.ds(start + late, rows), :] = given_ref[pl.ds(host * rows, rows), :]


def convolve_kernel(
    peers,
    lanes,
    early,
    in_refs,
    fore_ref,
    back_ref,
    wide_fore_ref,
    wide_back_ref,
    turn_fore_ref,
    turn_back_ref,
    out_ref,
    high_ref,
    low_ref,
):
    rows = 2 * lanes + 1
    inner = out_ref.shape[1]
    hosts = peers // 2
    chunk = 4

    def place(first, count=1):
        return pl.ds(first * peers, count * peers)

    def put(first, value):
        high, low = halves(value)
        here = pl.ds(first * peers, value.shape[0])
        high_ref[here, :] = high
        low_ref[here, :] = low

    def transformed(first, count, table_ref):
        high = high_ref[place(first, count), :]
        low = low_ref[place(first, count), :]
        high_table = table_ref[: 2 * inner, :]
        return dot(high, high_table) + dot(low, high_table) + dot(high, table_ref[2 * inner :, :])

    def rotated(real, imag, turn_ref):
        cosine, sine = turn_ref[0], turn_ref[1]
        return jnp.concatenate(
            [real * cosine - imag * sine, real * sine + imag * cosine], axis=1
        )

    def received(row):
        if len(in_refs) == 1:
            even = in_refs[0][pl.ds(row, hosts, stride=2 * rows), :]
            odd = in_refs[0][pl.ds(rows + row, hosts, stride=2 * rows), :]
        else:
            stride = 2 * rows - early
            even = in_refs[1][pl.ds(rows - early + row, hosts, stride=stride), :]
            if row < early:
                odd = in_refs[0][pl.ds(row, hosts, stride=early), :]
            else:
                odd = in_refs[1][pl.ds(row - early, hosts, stride=stride), :]
        return jnp.concatenate([even, odd], axis=0)

    fore = fore_ref[...]
    order = [2 * lanes] + list(range(2 * lanes))
    for start in range(0, rows, 2):
        chosen = order[start : start + 2]
        columns = []
        for row in chosen:
            high, low = halves(received(row))
            columns.append(jnp.concatenate([high, low, high], axis=0))
        spread = dot(fore, jnp.concatenate(columns, axis=1))
        for index, row in enumerate(chosen):
            part = spread[:, index * inner : (index + 1) * inner]
            put(row, rotated(part[:peers], part[peers:], turn_fore_ref))

    filt = transformed(2 * lanes, 1, wide_fore_ref)
    filt_re, filt_im = filt[:, :inner], filt[:, inner:]
    corr_re = jnp.zeros((peers, inner), f32)
    corr_im = jnp.zeros((peers, inner), f32)
    for first in range(0, lanes, chunk):
        gated = transformed(first, chunk, wide_fore_ref)
        grad = transformed(lanes + first, chunk, wide_fore_ref)
        for index in range(chunk):
            part = slice(index * peers, (index + 1) * peers)
            gated_re, gated_im = gated[part, :inner], gated[part, inner:]
            grad_re, grad_im = grad[part, :inner], grad[part, inner:]
            put(
                first + index,
                jnp.concatenate(
                    [
                        gated_re * filt_re - gated_im * filt_im,
                        gated_re * filt_im + gated_im * filt_re,
                    ],
                    axis=1,
                ),
            )
            put(
                lanes + first + index,
                jnp.concatenate(
                    [
                        filt_re * grad_re + filt_im * grad_im,
                        filt_re * grad_im - filt_im * grad_re,
                    ],
                    axis=1,
                ),
            )
            corr_re = corr_re + (gated_re * grad_re + gated_im * grad_im)
            corr_im = corr_im + (gated_re * grad_im - gated_im * grad_re)
    put(2 * lanes, jnp.concatenate([corr_re, corr_im], axis=1))

    for first in range(0, rows, 3):
        count = min(3, rows - first)
        spec = transformed(first, count, wide_back_ref)
        for index in range(count):
            part = spec[index * peers : (index + 1) * peers]
            put(first + index, rotated(part[:, :inner], part[:, inner:], turn_back_ref))

    back = back_ref[...]
    for start in range(0, rows, 2):
        columns = []
        for row in range(start, min(start + 2, rows)):
            high, low = high_ref[place(row), :], low_ref[place(row), :]
            high = jnp.concatenate([high[:, :inner], high[:, inner:]], axis=0)
            low = jnp.concatenate([low[:, :inner], low[:, inner:]], axis=0)
            columns.append(jnp.concatenate([high, low], axis=0))
        signal = dot(back, jnp.concatenate(columns, axis=1))
        signal = signal[:peers] + signal[peers:]
        for index in range(len(columns)):
            out_ref[pl.ds(start + index, peers, stride=rows), :] = signal[
                :, index * inner : (index + 1) * inner
            ]


def unpack_kernel(hosts, lanes, given, *refs):
    if given:
        in_ref, *refs = refs
        refs = refs[:4] + refs[9:]
    else:
        in_ref, *refs = refs
    key_ref, value_ref, grad_ref, query_ref, *refs = refs
    targets, kept, filter_ref, sems = refs[:5], refs[5:9], refs[9], refs[10]
    rows = 2 * lanes + 1
    half = hosts * lanes
    pairs = ((query_ref, grad_ref), (value_ref, key_ref))
    core = lax.rem(lax.axis_index("context"), 2)
    part = 1 - core if given else core
    place = pl.ds(pl.multiple_of(part * half, half), half)

    def finish(first, stride):
        filter_ref[...] = in_ref[pl.ds(first + 2 * lanes, hosts, stride=stride), :]
        copies = [
            pltpu.make_async_copy(
                filter_ref,
                targets[4].at[pl.ds(pl.multiple_of(part * hosts, hosts), hosts), :],
                sems.at[4],
            )
        ]
        copies[0].start()
        for index, pair in enumerate(pairs):
            for start in range(0, half, 128):
                blocks = []
                for offset in range(0, 128, lanes):
                    row = (start + offset) // lanes * stride + first + index * lanes
                    blocks.append(in_ref[pl.ds(row, lanes), :])
                signal = jnp.concatenate(blocks, axis=0).T
                columns = pl.ds(start, 128)
                for side, factor in enumerate(pair):
                    kept[2 * index + side][:, columns] = (
                        factor[:, columns].astype(f32) * signal
                    ).astype(bf16)
            for side in range(2):
                number = 2 * index + side
                copies.append(
                    pltpu.make_async_copy(
                        kept[number], targets[number].at[:, place], sems.at[number]
                    )
                )
                copies[-1].start()
        for copy in copies:
            copy.wait()

    if given:
        finish(0, rows)
        return

    @pl.when(core == 0)
    def _():
        finish(0, 2 * rows)

    @pl.when(core == 1)
    def _():
        finish(rows, 2 * rows)


def exchange(signal, groups):
    pieces = signal.reshape(signal.shape[0], 1, signal.shape[1])
    pieces = lax.all_to_all(pieces, "context", 0, 0, axis_index_groups=groups, tiled=True)
    return pieces.reshape(signal.shape)


def solution(mesh):
    peers = mesh.shape["context"]
    hosts = peers // 2
    groups = [[2 * host + core for host in range(hosts)] for core in range(2)]
    swap = [(rank, rank ^ 1) for rank in range(peers)]
    params = pltpu.CompilerParams(vmem_limit_bytes=48 * 1024 * 1024)
    early = 3

    def local(query_gate, key_gate, value_in, filter_raw, grad_out):
        inner, width = query_gate.shape
        lanes = width // filter_raw.shape[1]
        rows = 2 * lanes + 1
        scale = 1.0 / math.sqrt(peers * inner)
        constants = [jnp.asarray(table) for table in tables(peers, inner, scale)]

        def block_rows(count):
            return jax.ShapeDtypeStruct((hosts * count, inner), f32)

        held_half = pltpu.VMEM((inner, width // 2), bf16)
        half_scratch = [held_half] * 4 + [
            pltpu.VMEM((hosts, inner), f32),
            pltpu.SemaphoreType.DMA((5,)),
        ]
        half_wide = jax.ShapeDtypeStruct((inner, width // 2), bf16)
        sources = [
            pltpu.with_memory_space_constraint(array, pltpu.HBM)
            for array in (key_gate, value_in, grad_out, query_gate, filter_raw.T)
        ]

        def pack(other):
            return pl.pallas_call(
                lambda *refs: pack_kernel(hosts, lanes, other, *refs),
                out_shape=(block_rows(rows),) + (half_wide,) * 4,
                in_specs=[pl.BlockSpec(memory_space=pltpu.HBM)] * 5,
                scratch_shapes=half_scratch[4:],
                compiler_params=params,
                name="pack",
            )(*sources)

        other, *other_factors = pack(True)
        given = lax.ppermute(other, "context", swap)
        own, *own_factors = pack(False)

        def convolve(*held):
            count = len(held)
            return pl.pallas_call(
                lambda *refs: convolve_kernel(peers, lanes, early, refs[:count], *refs[count:]),
                out_shape=block_rows(2 * rows),
                scratch_shapes=[pltpu.VMEM((peers * rows, 2 * inner), bf16)] * 2,
                compiler_params=params,
                name="convolve",
            )(*held, *constants)

        def join(kernel, size, *parts):
            return pl.pallas_call(
                kernel, out_shape=block_rows(size), compiler_params=params, name="join"
            )(*parts)

        leads = lax.rem(lax.axis_index("context"), 2) == 0
        def lead(own, given):
            sent = join(lambda *refs: join_kernel(hosts, *refs), 2 * rows, own, given)
            return exchange(convolve(exchange(sent, groups)), groups)

        def follow(own, given):
            ahead = join(lambda *refs: take_kernel(hosts, 0, *refs), early, own)
            sent = join(
                lambda *refs: join_late_kernel(hosts, early, *refs), 2 * rows - early, own, given
            )
            held_ahead = exchange(ahead, groups)
            return exchange(convolve(held_ahead, exchange(sent, groups)), groups)

        back = lax.cond(leads, lead, follow, own, given)
        other_back = join(lambda *refs: take_other_kernel(hosts, *refs), rows, back)
        back_given = lax.ppermute(other_back, "context", swap)
        wide = jax.ShapeDtypeStruct((inner, width), bf16)
        shapes = (wide,) * 4 + (jax.ShapeDtypeStruct((peers, inner), f32),)
        hbm = pl.BlockSpec(memory_space=pltpu.HBM)
        vmem = pl.BlockSpec(memory_space=pltpu.VMEM)

        def unpack(given, signal, factors, *partial):
            return pl.pallas_call(
                lambda *refs: unpack_kernel(hosts, lanes, given, *refs),
                out_shape=shapes,
                in_specs=[vmem] * 5 + [hbm] * len(partial),
                out_specs=(hbm,) * 5,
                scratch_shapes=half_scratch,
                input_output_aliases={5 + index: index for index in range(len(partial))},
                compiler_params=params,
                name="unpack",
            )(signal, *factors, *partial)

        *outputs, grad_filter = unpack(
            True, back_given, other_factors, *unpack(False, back, own_factors)
        )
        return (*outputs, grad_filter.T)

    spec = P("context", "tensor")
    return jax.shard_map(
        local, mesh=mesh, in_specs=(spec,) * 5, out_specs=(spec,) * 5, check_vma=False
    )
```

```python
import math

import jax
import jax.numpy as jnp
import ml_dtypes
import numpy as np
from jax import lax
from jax.experimental import pallas as pl
from jax.experimental.pallas import tpu as pltpu
from jax.sharding import PartitionSpec as P

bf16 = jnp.bfloat16
f32 = jnp.float32


def split_table(table):
    high = table.astype(np.float32).astype(ml_dtypes.bfloat16)
    low = (table - high.astype(np.float64)).astype(np.float32).astype(ml_dtypes.bfloat16)
    return high, low


def tables(blocks, inner, scale):
    points = 2 * blocks * inner
    a = np.arange(blocks)
    b = np.arange(inner)
    odd = 2 * np.arange(blocks) + 1
    across = np.pi * np.outer(odd, a) / (2 * blocks)
    order = np.concatenate([np.arange(0, blocks, 2), np.arange(1, blocks, 2)])
    fore = np.concatenate([np.cos(across), -np.sin(across)], axis=0)[:, order]
    back = np.concatenate([np.cos(across), -np.sin(across)], axis=0).T
    fore_high, fore_low = split_table(fore)
    back_high, back_low = split_table(back)
    turn = np.pi * np.outer(odd, b) / points
    turn_fore = np.stack([np.cos(turn), -np.sin(turn)]).astype(np.float32)
    turn_back = (np.stack([np.cos(turn), np.sin(turn)]) * (2.0 * scale / points)).astype(np.float32)
    within = 2 * np.pi * np.outer(b, b) / inner
    cosine, sine = np.cos(within), np.sin(within)
    wide_fore = np.block([[cosine, -sine], [sine, cosine]])
    wide_back = np.block([[cosine, sine], [-sine, cosine]])
    fh, fl = split_table(wide_fore)
    bh, bl = split_table(wide_back)
    return (
        np.concatenate([fore_high, fore_high, fore_low], axis=1),
        np.block([[back_high, back_high], [back_low, np.zeros_like(back_low)]]),
        np.concatenate([fh, fl], axis=0),
        np.concatenate([bh, bl], axis=0),
        turn_fore,
        turn_back,
    )


def halves(value):
    high = value.astype(bf16)
    return high, (value - high.astype(f32)).astype(bf16)


def dot(left, right):
    return jnp.dot(left, right, preferred_element_type=f32)


def pack_kernel(hosts, lanes, other, *refs):
    sources, out_ref, targets, sems = refs[:5], refs[5], refs[6:11], refs[11]
    rows = 2 * lanes + 1
    half = hosts * lanes
    core = lax.rem(lax.axis_index("context"), 2)
    part = 1 - core if other else core
    columns = pl.ds(pl.multiple_of(part * half, half), half)
    copies = []
    for index in range(4):
        source = sources[index].at[:, columns]
        copies.append(pltpu.make_async_copy(source, targets[index], sems.at[index]))
    source = sources[4].at[pl.ds(pl.multiple_of(part * hosts, hosts), hosts), :]
    copies.append(pltpu.make_async_copy(source, targets[4], sems.at[4]))
    for copy in copies:
        copy.start()
    for index in range(2):
        copies[2 * index].wait()
        copies[2 * index + 1].wait()
        left, right = targets[2 * index], targets[2 * index + 1]
        for start in range(0, half, 128):
            place = pl.ds(start, 128)
            product = left[:, place].astype(f32) * right[:, place].astype(f32)
            turned = product.T
            for offset in range(0, 128, lanes):
                first = (start + offset) // lanes * rows + index * lanes
                out_ref[pl.ds(first, lanes), :] = turned[offset : offset + lanes]
    copies[4].wait()
    out_ref[pl.ds(2 * lanes, hosts, stride=rows), :] = targets[4][...]


def take_kernel(hosts, first, own_ref, out_ref):
    rows = own_ref.shape[0] // hosts
    count = out_ref.shape[0] // hosts
    for host in range(hosts):
        out_ref[pl.ds(host * count, count), :] = own_ref[pl.ds(host * rows + first, count), :]


def take_other_kernel(hosts, back_ref, out_ref):
    core = lax.rem(lax.axis_index("context"), 2)

    @pl.when(core == 0)
    def _():
        take_kernel(hosts, out_ref.shape[0] // hosts, back_ref, out_ref)

    @pl.when(core == 1)
    def _():
        take_kernel(hosts, 0, back_ref, out_ref)


def join_kernel(hosts, first_ref, second_ref, out_ref):
    rows = first_ref.shape[0] // hosts
    more = second_ref.shape[0] // hosts
    for host in range(hosts):
        start = host * (rows + more)
        out_ref[pl.ds(start, rows), :] = first_ref[pl.ds(host * rows, rows), :]
        out_ref[pl.ds(start + rows, more), :] = second_ref[pl.ds(host * more, more), :]


def join_late_kernel(hosts, early, own_ref, given_ref, out_ref):
    rows = own_ref.shape[0] // hosts
    late = rows - early
    for host in range(hosts):
        start = host * (rows + late)
        out_ref[pl.ds(start, late), :] = own_ref[pl.ds(host * rows + early, late), :]
        out_ref[pl.ds(start + late, rows), :] = given_ref[pl.ds(host * rows, rows), :]


def convolve_kernel(
    peers,
    lanes,
    early,
    in_refs,
    fore_ref,
    back_ref,
    wide_fore_ref,
    wide_back_ref,
    turn_fore_ref,
    turn_back_ref,
    out_ref,
    high_ref,
    low_ref,
):
    rows = 2 * lanes + 1
    inner = out_ref.shape[1]
    hosts = peers // 2
    chunk = 4

    def place(first, count=1):
        return pl.ds(first * peers, count * peers)

    def put(first, value):
        high, low = halves(value)
        here = pl.ds(first * peers, value.shape[0])
        high_ref[here, :] = high
        low_ref[here, :] = low

    def transformed(first, count, table_ref):
        high = high_ref[place(first, count), :]
        low = low_ref[place(first, count), :]
        high_table = table_ref[: 2 * inner, :]
        return dot(high, high_table) + dot(low, high_table) + dot(high, table_ref[2 * inner :, :])

    def rotated(real, imag, turn_ref):
        cosine, sine = turn_ref[0], turn_ref[1]
        return jnp.concatenate(
            [real * cosine - imag * sine, real * sine + imag * cosine], axis=1
        )

    def received(row):
        if len(in_refs) == 1:
            even = in_refs[0][pl.ds(row, hosts, stride=2 * rows), :]
            odd = in_refs[0][pl.ds(rows + row, hosts, stride=2 * rows), :]
        else:
            stride = 2 * rows - early
            even = in_refs[1][pl.ds(rows - early + row, hosts, stride=stride), :]
            if row < early:
                odd = in_refs[0][pl.ds(row, hosts, stride=early), :]
            else:
                odd = in_refs[1][pl.ds(row - early, hosts, stride=stride), :]
        return jnp.concatenate([even, odd], axis=0)

    fore = fore_ref[...]
    order = [2 * lanes] + list(range(2 * lanes))
    for start in range(0, rows, 2):
        chosen = order[start : start + 2]
        columns = []
        for row in chosen:
            high, low = halves(received(row))
            columns.append(jnp.concatenate([high, low, high], axis=0))
        spread = dot(fore, jnp.concatenate(columns, axis=1))
        for index, row in enumerate(chosen):
            part = spread[:, index * inner : (index + 1) * inner]
            put(row, rotated(part[:peers], part[peers:], turn_fore_ref))

    filt = transformed(2 * lanes, 1, wide_fore_ref)
    filt_re, filt_im = filt[:, :inner], filt[:, inner:]
    corr_re = jnp.zeros((peers, inner), f32)
    corr_im = jnp.zeros((peers, inner), f32)
    for first in range(0, lanes, chunk):
        gated = transformed(first, chunk, wide_fore_ref)
        grad = transformed(lanes + first, chunk, wide_fore_ref)
        for index in range(chunk):
            part = slice(index * peers, (index + 1) * peers)
            gated_re, gated_im = gated[part, :inner], gated[part, inner:]
            grad_re, grad_im = grad[part, :inner], grad[part, inner:]
            put(
                first + index,
                jnp.concatenate(
                    [
                        gated_re * filt_re - gated_im * filt_im,
                        gated_re * filt_im + gated_im * filt_re,
                    ],
                    axis=1,
                ),
            )
            put(
                lanes + first + index,
                jnp.concatenate(
                    [
                        filt_re * grad_re + filt_im * grad_im,
                        filt_re * grad_im - filt_im * grad_re,
                    ],
                    axis=1,
                ),
            )
            corr_re = corr_re + (gated_re * grad_re + gated_im * grad_im)
            corr_im = corr_im + (gated_re * grad_im - gated_im * grad_re)
    put(2 * lanes, jnp.concatenate([corr_re, corr_im], axis=1))

    for first in range(0, rows, 3):
        count = min(3, rows - first)
        spec = transformed(first, count, wide_back_ref)
        for index in range(count):
            part = spec[index * peers : (index + 1) * peers]
            put(first + index, rotated(part[:, :inner], part[:, inner:], turn_back_ref))

    back = back_ref[...]
    for start in range(0, rows, 2):
        columns = []
        for row in range(start, min(start + 2, rows)):
            high, low = high_ref[place(row), :], low_ref[place(row), :]
            high = jnp.concatenate([high[:, :inner], high[:, inner:]], axis=0)
            low = jnp.concatenate([low[:, :inner], low[:, inner:]], axis=0)
            columns.append(jnp.concatenate([high, low], axis=0))
        signal = dot(back, jnp.concatenate(columns, axis=1))
        signal = signal[:peers] + signal[peers:]
        for index in range(len(columns)):
            out_ref[pl.ds(start + index, peers, stride=rows), :] = signal[
                :, index * inner : (index + 1) * inner
            ]


def unpack_kernel(hosts, lanes, given, *refs):
    if given:
        in_ref, *refs = refs
        refs = refs[:4] + refs[9:]
    else:
        in_ref, *refs = refs
    key_ref, value_ref, grad_ref, query_ref, *refs = refs
    targets, kept, filter_ref, sems = refs[:5], refs[5:9], refs[9], refs[10]
    rows = 2 * lanes + 1
    half = hosts * lanes
    pairs = ((query_ref, grad_ref), (value_ref, key_ref))
    core = lax.rem(lax.axis_index("context"), 2)
    part = 1 - core if given else core
    place = pl.ds(pl.multiple_of(part * half, half), half)

    def finish(first, stride):
        filter_ref[...] = in_ref[pl.ds(first + 2 * lanes, hosts, stride=stride), :]
        copies = [
            pltpu.make_async_copy(
                filter_ref,
                targets[4].at[pl.ds(pl.multiple_of(part * hosts, hosts), hosts), :],
                sems.at[4],
            )
        ]
        copies[0].start()
        for index, pair in enumerate(pairs):
            for start in range(0, half, 128):
                blocks = []
                for offset in range(0, 128, lanes):
                    row = (start + offset) // lanes * stride + first + index * lanes
                    blocks.append(in_ref[pl.ds(row, lanes), :])
                signal = jnp.concatenate(blocks, axis=0).T
                columns = pl.ds(start, 128)
                for side, factor in enumerate(pair):
                    kept[2 * index + side][:, columns] = (
                        factor[:, columns].astype(f32) * signal
                    ).astype(bf16)
            for side in range(2):
                number = 2 * index + side
                copies.append(
                    pltpu.make_async_copy(
                        kept[number], targets[number].at[:, place], sems.at[number]
                    )
                )
                copies[-1].start()
        for copy in copies:
            copy.wait()

    if given:
        finish(0, rows)
        return

    @pl.when(core == 0)
    def _():
        finish(0, 2 * rows)

    @pl.when(core == 1)
    def _():
        finish(rows, 2 * rows)


def exchange(signal, groups):
    pieces = signal.reshape(signal.shape[0], 1, signal.shape[1])
    pieces = lax.all_to_all(pieces, "context", 0, 0, axis_index_groups=groups, tiled=True)
    return pieces.reshape(signal.shape)


def solution(mesh):
    peers = mesh.shape["context"]
    hosts = peers // 2
    groups = [[2 * host + core for host in range(hosts)] for core in range(2)]
    swap = [(rank, rank ^ 1) for rank in range(peers)]
    params = pltpu.CompilerParams(vmem_limit_bytes=48 * 1024 * 1024)
    early = 3

    def local(query_gate, key_gate, value_in, filter_raw, grad_out):
        inner, width = query_gate.shape
        lanes = width // filter_raw.shape[1]
        rows = 2 * lanes + 1
        scale = 1.0 / math.sqrt(peers * inner)
        constants = [jnp.asarray(table) for table in tables(peers, inner, scale)]

        def block_rows(count):
            return jax.ShapeDtypeStruct((hosts * count, inner), f32)

        held_half = pltpu.VMEM((inner, width // 2), bf16)
        half_scratch = [held_half] * 4 + [
            pltpu.VMEM((hosts, inner), f32),
            pltpu.SemaphoreType.DMA((5,)),
        ]
        half_wide = jax.ShapeDtypeStruct((inner, width // 2), bf16)
        sources = [
            pltpu.with_memory_space_constraint(array, pltpu.HBM)
            for array in (key_gate, value_in, grad_out, query_gate, filter_raw.T)
        ]

        def pack(other):
            return pl.pallas_call(
                lambda *refs: pack_kernel(hosts, lanes, other, *refs),
                out_shape=(block_rows(rows),) + (half_wide,) * 4,
                in_specs=[pl.BlockSpec(memory_space=pltpu.HBM)] * 5,
                scratch_shapes=half_scratch[4:],
                compiler_params=params,
                name="pack",
            )(*sources)

        other, *other_factors = pack(True)
        given = lax.ppermute(other, "context", swap)
        own, *own_factors = pack(False)

        def convolve(*held):
            count = len(held)
            return pl.pallas_call(
                lambda *refs: convolve_kernel(peers, lanes, early, refs[:count], *refs[count:]),
                out_shape=block_rows(2 * rows),
                scratch_shapes=[pltpu.VMEM((peers * rows, 2 * inner), bf16)] * 2,
                compiler_params=params,
                name="convolve",
            )(*held, *constants)

        def join(kernel, size, *parts):
            return pl.pallas_call(
                kernel, out_shape=block_rows(size), compiler_params=params, name="join"
            )(*parts)

        leads = lax.rem(lax.axis_index("context"), 2) == 0
        def lead(own, given):
            sent = join(lambda *refs: join_kernel(hosts, *refs), 2 * rows, own, given)
            return exchange(convolve(exchange(sent, groups)), groups)

        def follow(own, given):
            ahead = join(lambda *refs: take_kernel(hosts, 0, *refs), early, own)
            sent = join(
                lambda *refs: join_late_kernel(hosts, early, *refs), 2 * rows - early, own, given
            )
            held_ahead, sent = lax.optimization_barrier((exchange(ahead, groups), sent))
            return exchange(convolve(held_ahead, exchange(sent, groups)), groups)

        back = lax.cond(leads, lead, follow, own, given)
        other_back = join(lambda *refs: take_other_kernel(hosts, *refs), rows, back)
        back_given = lax.ppermute(other_back, "context", swap)
        wide = jax.ShapeDtypeStruct((inner, width), bf16)
        shapes = (wide,) * 4 + (jax.ShapeDtypeStruct((peers, inner), f32),)
        hbm = pl.BlockSpec(memory_space=pltpu.HBM)
        vmem = pl.BlockSpec(memory_space=pltpu.VMEM)

        def unpack(given, signal, factors, *partial):
            return pl.pallas_call(
                lambda *refs: unpack_kernel(hosts, lanes, given, *refs),
                out_shape=shapes,
                in_specs=[vmem] * 5 + [hbm] * len(partial),
                out_specs=(hbm,) * 5,
                scratch_shapes=half_scratch,
                input_output_aliases={5 + index: index for index in range(len(partial))},
                compiler_params=params,
                name="unpack",
            )(signal, *factors, *partial)

        *outputs, grad_filter = unpack(
            True, back_given, other_factors, *unpack(False, back, own_factors)
        )
        return (*outputs, grad_filter.T)

    spec = P("context", "tensor")
    return jax.shard_map(
        local, mesh=mesh, in_specs=(spec,) * 5, out_specs=(spec,) * 5, check_vma=False
    )
```

```python
import math

import jax
import jax.numpy as jnp
import ml_dtypes
import numpy as np
from jax import lax
from jax.experimental import pallas as pl
from jax.experimental.pallas import tpu as pltpu
from jax.sharding import PartitionSpec as P

bf16 = jnp.bfloat16
f32 = jnp.float32


def split_table(table):
    high = table.astype(np.float32).astype(ml_dtypes.bfloat16)
    low = (table - high.astype(np.float64)).astype(np.float32).astype(ml_dtypes.bfloat16)
    return high, low


def tables(blocks, inner, scale):
    points = 2 * blocks * inner
    a = np.arange(blocks)
    b = np.arange(inner)
    odd = 2 * np.arange(blocks) + 1
    across = np.pi * np.outer(odd, a) / (2 * blocks)
    order = np.concatenate([np.arange(0, blocks, 2), np.arange(1, blocks, 2)])
    fore = np.concatenate([np.cos(across), -np.sin(across)], axis=0)[:, order]
    back = np.concatenate([np.cos(across), -np.sin(across)], axis=0).T
    fore_high, fore_low = split_table(fore)
    back_high, back_low = split_table(back)
    turn = np.pi * np.outer(odd, b) / points
    turn_fore = np.stack([np.cos(turn), -np.sin(turn)]).astype(np.float32)
    turn_back = (np.stack([np.cos(turn), np.sin(turn)]) * (2.0 * scale / points)).astype(np.float32)
    within = 2 * np.pi * np.outer(b, b) / inner
    cosine, sine = np.cos(within), np.sin(within)
    wide_fore = np.block([[cosine, -sine], [sine, cosine]])
    wide_back = np.block([[cosine, sine], [-sine, cosine]])
    fh, fl = split_table(wide_fore)
    bh, bl = split_table(wide_back)
    return (
        np.concatenate([fore_high, fore_high, fore_low], axis=1),
        np.block([[back_high, back_high], [back_low, np.zeros_like(back_low)]]),
        np.concatenate([fh, fl], axis=0),
        np.concatenate([bh, bl], axis=0),
        turn_fore,
        turn_back,
    )


def halves(value):
    high = value.astype(bf16)
    return high, (value - high.astype(f32)).astype(bf16)


def dot(left, right):
    return jnp.dot(left, right, preferred_element_type=f32)


def pack_kernel(hosts, lanes, other, *refs):
    sources, sems = refs[:5], refs[-1]
    outs, targets = refs[5:-6], refs[-6:-1]
    first_rows = (0, lanes) if other else (0, 0)
    rows = 2 * lanes + 1
    half = hosts * lanes
    core = lax.rem(lax.axis_index("context"), 2)
    part = 1 - core if other else core
    columns = pl.ds(pl.multiple_of(part * half, half), half)
    copies = []
    for index in range(4):
        source = sources[index].at[:, columns]
        copies.append(pltpu.make_async_copy(source, targets[index], sems.at[index]))
    source = sources[4].at[pl.ds(pl.multiple_of(part * hosts, hosts), hosts), :]
    copies.append(pltpu.make_async_copy(source, targets[4], sems.at[4]))
    for copy in copies:
        copy.start()
    for index in range(2):
        copies[2 * index].wait()
        copies[2 * index + 1].wait()
        left, right = targets[2 * index], targets[2 * index + 1]
        for start in range(0, half, 128):
            place = pl.ds(start, 128)
            product = left[:, place].astype(f32) * right[:, place].astype(f32)
            turned = product.T
            for offset in range(0, 128, lanes):
                out_ref = outs[index] if other else outs[0]
                stride = out_ref.shape[0] // hosts
                first = (start + offset) // lanes * stride + index * lanes - first_rows[index]
                out_ref[pl.ds(first, lanes), :] = turned[offset : offset + lanes]
    copies[4].wait()
    out_ref = outs[1] if other else outs[0]
    stride = out_ref.shape[0] // hosts
    out_ref[pl.ds(stride - 1, hosts, stride=stride), :] = targets[4][...]


def take_kernel(hosts, first, own_ref, out_ref):
    rows = own_ref.shape[0] // hosts
    count = out_ref.shape[0] // hosts
    for host in range(hosts):
        out_ref[pl.ds(host * count, count), :] = own_ref[pl.ds(host * rows + first, count), :]


def take_other_kernel(hosts, back_ref, out_ref):
    core = lax.rem(lax.axis_index("context"), 2)

    @pl.when(core == 0)
    def _():
        take_kernel(hosts, out_ref.shape[0] // hosts, back_ref, out_ref)

    @pl.when(core == 1)
    def _():
        take_kernel(hosts, 0, back_ref, out_ref)


def join_kernel(hosts, skipped, *refs):
    *parts, out_ref = refs
    total = out_ref.shape[0] // hosts
    for host in range(hosts):
        start = host * total
        for index, part in enumerate(parts):
            rows = part.shape[0] // hosts
            skip = 0 if index else skipped
            out_ref[pl.ds(start, rows - skip), :] = part[pl.ds(host * rows + skip, rows - skip), :]
            start += rows - skip


def convolve_kernel(
    peers,
    lanes,
    early,
    in_refs,
    fore_ref,
    back_ref,
    wide_fore_ref,
    wide_back_ref,
    turn_fore_ref,
    turn_back_ref,
    out_ref,
    high_ref,
    low_ref,
):
    rows = 2 * lanes + 1
    inner = out_ref.shape[1]
    hosts = peers // 2
    chunk = 4

    def place(first, count=1):
        return pl.ds(first * peers, count * peers)

    def put(first, value):
        high, low = halves(value)
        here = pl.ds(first * peers, value.shape[0])
        high_ref[here, :] = high
        low_ref[here, :] = low

    def transformed(first, count, table_ref):
        high = high_ref[place(first, count), :]
        low = low_ref[place(first, count), :]
        high_table = table_ref[: 2 * inner, :]
        return dot(high, high_table) + dot(low, high_table) + dot(high, table_ref[2 * inner :, :])

    def rotated(real, imag, turn_ref):
        cosine, sine = turn_ref[0], turn_ref[1]
        return jnp.concatenate(
            [real * cosine - imag * sine, real * sine + imag * cosine], axis=1
        )

    def received(row):
        if len(in_refs) == 1:
            even = in_refs[0][pl.ds(row, hosts, stride=2 * rows), :]
            odd = in_refs[0][pl.ds(rows + row, hosts, stride=2 * rows), :]
        else:
            stride = 2 * rows - early
            even = in_refs[1][pl.ds(rows - early + row, hosts, stride=stride), :]
            if row < early:
                odd = in_refs[0][pl.ds(row, hosts, stride=early), :]
            else:
                odd = in_refs[1][pl.ds(row - early, hosts, stride=stride), :]
        return jnp.concatenate([even, odd], axis=0)

    fore = fore_ref[...]
    order = [2 * lanes] + list(range(2 * lanes))
    for start in range(0, rows, 2):
        chosen = order[start : start + 2]
        columns = []
        for row in chosen:
            high, low = halves(received(row))
            columns.append(jnp.concatenate([high, low, high], axis=0))
        spread = dot(fore, jnp.concatenate(columns, axis=1))
        for index, row in enumerate(chosen):
            part = spread[:, index * inner : (index + 1) * inner]
            put(row, rotated(part[:peers], part[peers:], turn_fore_ref))

    filt = transformed(2 * lanes, 1, wide_fore_ref)
    filt_re, filt_im = filt[:, :inner], filt[:, inner:]
    corr_re = jnp.zeros((peers, inner), f32)
    corr_im = jnp.zeros((peers, inner), f32)
    for first in range(0, lanes, chunk):
        gated = transformed(first, chunk, wide_fore_ref)
        grad = transformed(lanes + first, chunk, wide_fore_ref)
        for index in range(chunk):
            part = slice(index * peers, (index + 1) * peers)
            gated_re, gated_im = gated[part, :inner], gated[part, inner:]
            grad_re, grad_im = grad[part, :inner], grad[part, inner:]
            put(
                first + index,
                jnp.concatenate(
                    [
                        gated_re * filt_re - gated_im * filt_im,
                        gated_re * filt_im + gated_im * filt_re,
                    ],
                    axis=1,
                ),
            )
            put(
                lanes + first + index,
                jnp.concatenate(
                    [
                        filt_re * grad_re + filt_im * grad_im,
                        filt_re * grad_im - filt_im * grad_re,
                    ],
                    axis=1,
                ),
            )
            corr_re = corr_re + (gated_re * grad_re + gated_im * grad_im)
            corr_im = corr_im + (gated_re * grad_im - gated_im * grad_re)
    put(2 * lanes, jnp.concatenate([corr_re, corr_im], axis=1))

    for first in range(0, rows, 3):
        count = min(3, rows - first)
        spec = transformed(first, count, wide_back_ref)
        for index in range(count):
            part = spec[index * peers : (index + 1) * peers]
            put(first + index, rotated(part[:, :inner], part[:, inner:], turn_back_ref))

    back = back_ref[...]
    for start in range(0, rows, 2):
        columns = []
        for row in range(start, min(start + 2, rows)):
            high, low = high_ref[place(row), :], low_ref[place(row), :]
            high = jnp.concatenate([high[:, :inner], high[:, inner:]], axis=0)
            low = jnp.concatenate([low[:, :inner], low[:, inner:]], axis=0)
            columns.append(jnp.concatenate([high, low], axis=0))
        signal = dot(back, jnp.concatenate(columns, axis=1))
        signal = signal[:peers] + signal[peers:]
        for index in range(len(columns)):
            out_ref[pl.ds(start + index, peers, stride=rows), :] = signal[
                :, index * inner : (index + 1) * inner
            ]


def unpack_kernel(hosts, lanes, given, *refs):
    if given:
        in_ref, *refs = refs
        refs = refs[:4] + refs[9:]
    else:
        in_ref, *refs = refs
    key_ref, value_ref, grad_ref, query_ref, *refs = refs
    targets, kept, filter_ref, sems = refs[:5], refs[5:9], refs[9], refs[10]
    rows = 2 * lanes + 1
    half = hosts * lanes
    pairs = ((query_ref, grad_ref), (value_ref, key_ref))
    core = lax.rem(lax.axis_index("context"), 2)
    part = 1 - core if given else core
    place = pl.ds(pl.multiple_of(part * half, half), half)

    def finish(first, stride):
        filter_ref[...] = in_ref[pl.ds(first + 2 * lanes, hosts, stride=stride), :]
        copies = [
            pltpu.make_async_copy(
                filter_ref,
                targets[4].at[pl.ds(pl.multiple_of(part * hosts, hosts), hosts), :],
                sems.at[4],
            )
        ]
        copies[0].start()
        for index, pair in enumerate(pairs):
            for start in range(0, half, 128):
                blocks = []
                for offset in range(0, 128, lanes):
                    row = (start + offset) // lanes * stride + first + index * lanes
                    blocks.append(in_ref[pl.ds(row, lanes), :])
                signal = jnp.concatenate(blocks, axis=0).T
                columns = pl.ds(start, 128)
                for side, factor in enumerate(pair):
                    kept[2 * index + side][:, columns] = (
                        factor[:, columns].astype(f32) * signal
                    ).astype(bf16)
            for side in range(2):
                number = 2 * index + side
                copies.append(
                    pltpu.make_async_copy(
                        kept[number], targets[number].at[:, place], sems.at[number]
                    )
                )
                copies[-1].start()
        for copy in copies:
            copy.wait()

    if given:
        finish(0, rows)
        return

    @pl.when(core == 0)
    def _():
        finish(0, 2 * rows)

    @pl.when(core == 1)
    def _():
        finish(rows, 2 * rows)


def exchange(signal, groups):
    pieces = signal.reshape(signal.shape[0], 1, signal.shape[1])
    pieces = lax.all_to_all(pieces, "context", 0, 0, axis_index_groups=groups, tiled=True)
    return pieces.reshape(signal.shape)


def solution(mesh):
    peers = mesh.shape["context"]
    hosts = peers // 2
    groups = [[2 * host + core for host in range(hosts)] for core in range(2)]
    swap = [(rank, rank ^ 1) for rank in range(peers)]
    params = pltpu.CompilerParams(vmem_limit_bytes=48 * 1024 * 1024)
    early = 3

    def local(query_gate, key_gate, value_in, filter_raw, grad_out):
        inner, width = query_gate.shape
        lanes = width // filter_raw.shape[1]
        rows = 2 * lanes + 1
        scale = 1.0 / math.sqrt(peers * inner)
        constants = [jnp.asarray(table) for table in tables(peers, inner, scale)]

        def block_rows(count):
            return jax.ShapeDtypeStruct((hosts * count, inner), f32)

        held_half = pltpu.VMEM((inner, width // 2), bf16)
        half_scratch = [held_half] * 4 + [
            pltpu.VMEM((hosts, inner), f32),
            pltpu.SemaphoreType.DMA((5,)),
        ]
        half_wide = jax.ShapeDtypeStruct((inner, width // 2), bf16)
        sources = [
            pltpu.with_memory_space_constraint(array, pltpu.HBM)
            for array in (key_gate, value_in, grad_out, query_gate, filter_raw.T)
        ]

        def pack(other):
            return pl.pallas_call(
                lambda *refs: pack_kernel(hosts, lanes, other, *refs),
                out_shape=(
                    (block_rows(lanes), block_rows(lanes + 1)) if other else (block_rows(rows),)
                )
                + (half_wide,) * 4,
                in_specs=[pl.BlockSpec(memory_space=pltpu.HBM)] * 5,
                scratch_shapes=half_scratch[4:],
                compiler_params=params,
                name="pack",
            )(*sources)

        other_gated, other_grad, *other_factors = pack(True)
        given_gated = lax.ppermute(other_gated, "context", swap)
        given_grad = lax.ppermute(other_grad, "context", swap)
        own, *own_factors = pack(False)

        def convolve(*held):
            count = len(held)
            return pl.pallas_call(
                lambda *refs: convolve_kernel(peers, lanes, early, refs[:count], *refs[count:]),
                out_shape=block_rows(2 * rows),
                scratch_shapes=[pltpu.VMEM((peers * rows, 2 * inner), bf16)] * 2,
                compiler_params=params,
                name="convolve",
            )(*held, *constants)

        def join(kernel, size, *parts):
            return pl.pallas_call(
                kernel, out_shape=block_rows(size), compiler_params=params, name="join"
            )(*parts)

        leads = lax.rem(lax.axis_index("context"), 2) == 0
        def lead(*parts):
            sent = join(lambda *refs: join_kernel(hosts, 0, *refs), 2 * rows, *parts)
            return exchange(convolve(exchange(sent, groups)), groups)

        def follow(own, *given):
            ahead = join(lambda *refs: take_kernel(hosts, 0, *refs), early, own)
            sent = join(
                lambda *refs: join_kernel(hosts, early, *refs), 2 * rows - early, own, *given
            )
            held_ahead, sent = lax.optimization_barrier((exchange(ahead, groups), sent))
            return exchange(convolve(held_ahead, exchange(sent, groups)), groups)

        back = lax.cond(leads, lead, follow, own, given_gated, given_grad)
        other_back = join(lambda *refs: take_other_kernel(hosts, *refs), rows, back)
        back_given = lax.ppermute(other_back, "context", swap)
        wide = jax.ShapeDtypeStruct((inner, width), bf16)
        shapes = (wide,) * 4 + (jax.ShapeDtypeStruct((peers, inner), f32),)
        hbm = pl.BlockSpec(memory_space=pltpu.HBM)
        vmem = pl.BlockSpec(memory_space=pltpu.VMEM)

        def unpack(given, signal, factors, *partial):
            return pl.pallas_call(
                lambda *refs: unpack_kernel(hosts, lanes, given, *refs),
                out_shape=shapes,
                in_specs=[vmem] * 5 + [hbm] * len(partial),
                out_specs=(hbm,) * 5,
                scratch_shapes=half_scratch,
                input_output_aliases={5 + index: index for index in range(len(partial))},
                compiler_params=params,
                name="unpack",
            )(signal, *factors, *partial)

        *outputs, grad_filter = unpack(
            True, back_given, other_factors, *unpack(False, back, own_factors)
        )
        return (*outputs, grad_filter.T)

    spec = P("context", "tensor")
    return jax.shard_map(
        local, mesh=mesh, in_specs=(spec,) * 5, out_specs=(spec,) * 5, check_vma=False
    )
```

```python
import math

import jax
import jax.numpy as jnp
import ml_dtypes
import numpy as np
from jax import lax
from jax.experimental import pallas as pl
from jax.experimental.pallas import tpu as pltpu
from jax.sharding import PartitionSpec as P

bf16 = jnp.bfloat16
f32 = jnp.float32


def split_table(table):
    high = table.astype(np.float32).astype(ml_dtypes.bfloat16)
    low = (table - high.astype(np.float64)).astype(np.float32).astype(ml_dtypes.bfloat16)
    return high, low


def tables(blocks, inner, scale):
    points = 2 * blocks * inner
    a = np.arange(blocks)
    b = np.arange(inner)
    odd = 2 * np.arange(blocks) + 1
    across = np.pi * np.outer(odd, a) / (2 * blocks)
    order = np.concatenate([np.arange(0, blocks, 2), np.arange(1, blocks, 2)])
    fore = np.concatenate([np.cos(across), -np.sin(across)], axis=0)[:, order]
    back = np.concatenate([np.cos(across), -np.sin(across)], axis=0).T
    fore_high, fore_low = split_table(fore)
    back_high, back_low = split_table(back)
    turn = np.pi * np.outer(odd, b) / points
    turn_fore = np.stack([np.cos(turn), -np.sin(turn)]).astype(np.float32)
    turn_back = (np.stack([np.cos(turn), np.sin(turn)]) * (2.0 * scale / points)).astype(np.float32)
    within = 2 * np.pi * np.outer(b, b) / inner
    cosine, sine = np.cos(within), np.sin(within)
    wide_fore = np.block([[cosine, -sine], [sine, cosine]])
    wide_back = np.block([[cosine, sine], [-sine, cosine]])
    fh, fl = split_table(wide_fore)
    bh, bl = split_table(wide_back)
    return (
        np.concatenate([fore_high, fore_high, fore_low], axis=1),
        np.block([[back_high, back_high], [back_low, np.zeros_like(back_low)]]),
        np.concatenate([fh, fl], axis=0),
        np.concatenate([bh, bl], axis=0),
        turn_fore,
        turn_back,
    )


def halves(value):
    high = value.astype(bf16)
    return high, (value - high.astype(f32)).astype(bf16)


def dot(left, right):
    return jnp.dot(left, right, preferred_element_type=f32)


def pack_rows(hosts, lanes, factors, outs, ready):
    rows = 2 * lanes + 1
    for index in range(2):
        ready(index)
        left, right = factors[2 * index], factors[2 * index + 1]
        out_ref = outs[index % len(outs)]
        stride = out_ref.shape[0] // hosts
        skip = index * lanes if stride == rows else 0
        for start in range(0, hosts * lanes, 128):
            place = pl.ds(start, 128)
            turned = (left[:, place].astype(f32) * right[:, place].astype(f32)).T
            for offset in range(0, 128, lanes):
                first = (start + offset) // lanes * stride + skip
                out_ref[pl.ds(first, lanes), :] = turned[offset : offset + lanes]


def pack_filter(hosts, part, filter_hbm, filter_ref, sem):
    rows = pl.ds(pl.multiple_of(part * hosts, hosts), hosts)
    return pltpu.make_async_copy(filter_hbm.at[rows, :], filter_ref, sem)


def pack_other_kernel(hosts, lanes, *refs):
    sources, outs, other, own, filter_ref, sems = (
        refs[:5],
        refs[5:7],
        refs[7:11],
        refs[11:15],
        refs[15],
        refs[16],
    )
    half = hosts * lanes
    core = lax.rem(lax.axis_index("context"), 2)
    copies = []
    for number, (targets, part) in enumerate(((other, 1 - core), (own, core))):
        columns = pl.ds(pl.multiple_of(part * half, half), half)
        for index in range(4):
            source = sources[index].at[:, columns]
            copies.append(
                pltpu.make_async_copy(source, targets[index], sems.at[4 * number + index])
            )
    copies.append(pack_filter(hosts, 1 - core, sources[4], filter_ref, sems.at[8]))
    for copy in copies:
        copy.start()

    def ready(index):
        copies[2 * index].wait()
        copies[2 * index + 1].wait()

    pack_rows(hosts, lanes, other, outs, ready)
    copies[8].wait()
    stride = outs[1].shape[0] // hosts
    outs[1][pl.ds(stride - 1, hosts, stride=stride), :] = filter_ref[...]
    for copy in copies[4:8]:
        copy.wait()


def pack_own_kernel(hosts, lanes, *refs):
    factors, filter_hbm, out_ref, filter_ref, sems = refs[:4], refs[4], refs[5], refs[6], refs[7]
    core = lax.rem(lax.axis_index("context"), 2)
    copy = pack_filter(hosts, core, filter_hbm, filter_ref, sems.at[0])
    copy.start()
    pack_rows(hosts, lanes, factors, (out_ref,), lambda index: None)
    copy.wait()
    stride = out_ref.shape[0] // hosts
    out_ref[pl.ds(stride - 1, hosts, stride=stride), :] = filter_ref[...]


def take_kernel(hosts, first, own_ref, out_ref):
    rows = own_ref.shape[0] // hosts
    count = out_ref.shape[0] // hosts
    for host in range(hosts):
        out_ref[pl.ds(host * count, count), :] = own_ref[pl.ds(host * rows + first, count), :]


def take_other_kernel(hosts, back_ref, out_ref):
    core = lax.rem(lax.axis_index("context"), 2)

    @pl.when(core == 0)
    def _():
        take_kernel(hosts, out_ref.shape[0] // hosts, back_ref, out_ref)

    @pl.when(core == 1)
    def _():
        take_kernel(hosts, 0, back_ref, out_ref)


def join_kernel(hosts, skipped, *refs):
    *parts, out_ref = refs
    total = out_ref.shape[0] // hosts
    for host in range(hosts):
        start = host * total
        for index, part in enumerate(parts):
            rows = part.shape[0] // hosts
            skip = 0 if index else skipped
            out_ref[pl.ds(start, rows - skip), :] = part[pl.ds(host * rows + skip, rows - skip), :]
            start += rows - skip


def convolve_kernel(
    peers,
    lanes,
    early,
    in_refs,
    fore_ref,
    back_ref,
    wide_fore_ref,
    wide_back_ref,
    turn_fore_ref,
    turn_back_ref,
    out_ref,
    high_ref,
    low_ref,
):
    rows = 2 * lanes + 1
    inner = out_ref.shape[1]
    hosts = peers // 2
    chunk = 4

    def place(first, count=1):
        return pl.ds(first * peers, count * peers)

    def put(first, value):
        high, low = halves(value)
        here = pl.ds(first * peers, value.shape[0])
        high_ref[here, :] = high
        low_ref[here, :] = low

    def transformed(first, count, table_ref):
        high = high_ref[place(first, count), :]
        low = low_ref[place(first, count), :]
        high_table = table_ref[: 2 * inner, :]
        return dot(high, high_table) + dot(low, high_table) + dot(high, table_ref[2 * inner :, :])

    def rotated(real, imag, turn_ref):
        cosine, sine = turn_ref[0], turn_ref[1]
        return jnp.concatenate(
            [real * cosine - imag * sine, real * sine + imag * cosine], axis=1
        )

    def received(row):
        if len(in_refs) == 1:
            even = in_refs[0][pl.ds(row, hosts, stride=2 * rows), :]
            odd = in_refs[0][pl.ds(rows + row, hosts, stride=2 * rows), :]
        else:
            stride = 2 * rows - early
            even = in_refs[1][pl.ds(rows - early + row, hosts, stride=stride), :]
            if row < early:
                odd = in_refs[0][pl.ds(row, hosts, stride=early), :]
            else:
                odd = in_refs[1][pl.ds(row - early, hosts, stride=stride), :]
        return jnp.concatenate([even, odd], axis=0)

    fore = fore_ref[...]
    order = [2 * lanes] + list(range(2 * lanes))
    for start in range(0, rows, 2):
        chosen = order[start : start + 2]
        columns = []
        for row in chosen:
            high, low = halves(received(row))
            columns.append(jnp.concatenate([high, low, high], axis=0))
        spread = dot(fore, jnp.concatenate(columns, axis=1))
        for index, row in enumerate(chosen):
            part = spread[:, index * inner : (index + 1) * inner]
            put(row, rotated(part[:peers], part[peers:], turn_fore_ref))

    filt = transformed(2 * lanes, 1, wide_fore_ref)
    filt_re, filt_im = filt[:, :inner], filt[:, inner:]
    corr_re = jnp.zeros((peers, inner), f32)
    corr_im = jnp.zeros((peers, inner), f32)
    for first in range(0, lanes, chunk):
        gated = transformed(first, chunk, wide_fore_ref)
        grad = transformed(lanes + first, chunk, wide_fore_ref)
        for index in range(chunk):
            part = slice(index * peers, (index + 1) * peers)
            gated_re, gated_im = gated[part, :inner], gated[part, inner:]
            grad_re, grad_im = grad[part, :inner], grad[part, inner:]
            put(
                first + index,
                jnp.concatenate(
                    [
                        gated_re * filt_re - gated_im * filt_im,
                        gated_re * filt_im + gated_im * filt_re,
                    ],
                    axis=1,
                ),
            )
            put(
                lanes + first + index,
                jnp.concatenate(
                    [
                        filt_re * grad_re + filt_im * grad_im,
                        filt_re * grad_im - filt_im * grad_re,
                    ],
                    axis=1,
                ),
            )
            corr_re = corr_re + (gated_re * grad_re + gated_im * grad_im)
            corr_im = corr_im + (gated_re * grad_im - gated_im * grad_re)
    put(2 * lanes, jnp.concatenate([corr_re, corr_im], axis=1))

    for first in range(0, rows, 3):
        count = min(3, rows - first)
        spec = transformed(first, count, wide_back_ref)
        for index in range(count):
            part = spec[index * peers : (index + 1) * peers]
            put(first + index, rotated(part[:, :inner], part[:, inner:], turn_back_ref))

    back = back_ref[...]
    for start in range(0, rows, 2):
        columns = []
        for row in range(start, min(start + 2, rows)):
            high, low = high_ref[place(row), :], low_ref[place(row), :]
            high = jnp.concatenate([high[:, :inner], high[:, inner:]], axis=0)
            low = jnp.concatenate([low[:, :inner], low[:, inner:]], axis=0)
            columns.append(jnp.concatenate([high, low], axis=0))
        signal = dot(back, jnp.concatenate(columns, axis=1))
        signal = signal[:peers] + signal[peers:]
        for index in range(len(columns)):
            out_ref[pl.ds(start + index, peers, stride=rows), :] = signal[
                :, index * inner : (index + 1) * inner
            ]


def unpack_kernel(hosts, lanes, given, *refs):
    if given:
        in_ref, *refs = refs
        refs = refs[:4] + refs[9:]
    else:
        in_ref, *refs = refs
    key_ref, value_ref, grad_ref, query_ref, *refs = refs
    targets, kept, filter_ref, sems = refs[:5], refs[5:9], refs[9], refs[10]
    rows = 2 * lanes + 1
    half = hosts * lanes
    pairs = ((query_ref, grad_ref), (value_ref, key_ref))
    core = lax.rem(lax.axis_index("context"), 2)
    part = 1 - core if given else core
    place = pl.ds(pl.multiple_of(part * half, half), half)

    def finish(first, stride):
        filter_ref[...] = in_ref[pl.ds(first + 2 * lanes, hosts, stride=stride), :]
        copies = [
            pltpu.make_async_copy(
                filter_ref,
                targets[4].at[pl.ds(pl.multiple_of(part * hosts, hosts), hosts), :],
                sems.at[4],
            )
        ]
        copies[0].start()
        for index, pair in enumerate(pairs):
            for start in range(0, half, 128):
                blocks = []
                for offset in range(0, 128, lanes):
                    row = (start + offset) // lanes * stride + first + index * lanes
                    blocks.append(in_ref[pl.ds(row, lanes), :])
                signal = jnp.concatenate(blocks, axis=0).T
                columns = pl.ds(start, 128)
                for side, factor in enumerate(pair):
                    kept[2 * index + side][:, columns] = (
                        factor[:, columns].astype(f32) * signal
                    ).astype(bf16)
            for side in range(2):
                number = 2 * index + side
                copies.append(
                    pltpu.make_async_copy(
                        kept[number], targets[number].at[:, place], sems.at[number]
                    )
                )
                copies[-1].start()
        for copy in copies:
            copy.wait()

    if given:
        finish(0, rows)
        return

    @pl.when(core == 0)
    def _():
        finish(0, 2 * rows)

    @pl.when(core == 1)
    def _():
        finish(rows, 2 * rows)


def exchange(signal, groups):
    pieces = signal.reshape(signal.shape[0], 1, signal.shape[1])
    pieces = lax.all_to_all(pieces, "context", 0, 0, axis_index_groups=groups, tiled=True)
    return pieces.reshape(signal.shape)


def solution(mesh):
    peers = mesh.shape["context"]
    hosts = peers // 2
    groups = [[2 * host + core for host in range(hosts)] for core in range(2)]
    swap = [(rank, rank ^ 1) for rank in range(peers)]
    params = pltpu.CompilerParams(vmem_limit_bytes=48 * 1024 * 1024)
    early = 3

    def local(query_gate, key_gate, value_in, filter_raw, grad_out):
        inner, width = query_gate.shape
        lanes = width // filter_raw.shape[1]
        rows = 2 * lanes + 1
        scale = 1.0 / math.sqrt(peers * inner)
        constants = [jnp.asarray(table) for table in tables(peers, inner, scale)]

        def block_rows(count):
            return jax.ShapeDtypeStruct((hosts * count, inner), f32)

        held_half = pltpu.VMEM((inner, width // 2), bf16)
        half_scratch = [held_half] * 4 + [
            pltpu.VMEM((hosts, inner), f32),
            pltpu.SemaphoreType.DMA((5,)),
        ]
        half_wide = jax.ShapeDtypeStruct((inner, width // 2), bf16)
        sources = [
            pltpu.with_memory_space_constraint(array, pltpu.HBM)
            for array in (key_gate, value_in, grad_out, query_gate, filter_raw.T)
        ]

        hbm = pl.BlockSpec(memory_space=pltpu.HBM)
        vmem = pl.BlockSpec(memory_space=pltpu.VMEM)
        filter_half = pltpu.VMEM((hosts, inner), f32)
        other_gated, other_grad, *factors = pl.pallas_call(
            lambda *refs: pack_other_kernel(hosts, lanes, *refs),
            out_shape=(block_rows(lanes), block_rows(lanes + 1)) + (half_wide,) * 8,
            in_specs=[hbm] * 5,
            scratch_shapes=[filter_half, pltpu.SemaphoreType.DMA((9,))],
            compiler_params=params,
            name="pack_other",
        )(*sources)
        other_factors, own_factors = factors[:4], factors[4:]
        given_gated = lax.ppermute(other_gated, "context", swap)
        given_grad = lax.ppermute(other_grad, "context", swap)
        own = pl.pallas_call(
            lambda *refs: pack_own_kernel(hosts, lanes, *refs),
            out_shape=block_rows(rows),
            in_specs=[vmem] * 4 + [hbm],
            scratch_shapes=[filter_half, pltpu.SemaphoreType.DMA((1,))],
            compiler_params=params,
            name="pack_own",
        )(*own_factors, sources[4])

        def convolve(*held):
            count = len(held)
            return pl.pallas_call(
                lambda *refs: convolve_kernel(peers, lanes, early, refs[:count], *refs[count:]),
                out_shape=block_rows(2 * rows),
                scratch_shapes=[pltpu.VMEM((peers * rows, 2 * inner), bf16)] * 2,
                compiler_params=params,
                name="convolve",
            )(*held, *constants)

        def join(kernel, size, *parts):
            return pl.pallas_call(
                kernel, out_shape=block_rows(size), compiler_params=params, name="join"
            )(*parts)

        leads = lax.rem(lax.axis_index("context"), 2) == 0
        def lead(*parts):
            sent = join(lambda *refs: join_kernel(hosts, 0, *refs), 2 * rows, *parts)
            return exchange(convolve(exchange(sent, groups)), groups)

        def follow(own, *given):
            ahead = join(lambda *refs: take_kernel(hosts, 0, *refs), early, own)
            sent = join(
                lambda *refs: join_kernel(hosts, early, *refs), 2 * rows - early, own, *given
            )
            held_ahead, sent = lax.optimization_barrier((exchange(ahead, groups), sent))
            return exchange(convolve(held_ahead, exchange(sent, groups)), groups)

        back = lax.cond(leads, lead, follow, own, given_gated, given_grad)
        other_back = join(lambda *refs: take_other_kernel(hosts, *refs), rows, back)
        back_given = lax.ppermute(other_back, "context", swap)
        wide = jax.ShapeDtypeStruct((inner, width), bf16)
        shapes = (wide,) * 4 + (jax.ShapeDtypeStruct((peers, inner), f32),)
        hbm = pl.BlockSpec(memory_space=pltpu.HBM)
        vmem = pl.BlockSpec(memory_space=pltpu.VMEM)

        def unpack(given, signal, factors, *partial):
            return pl.pallas_call(
                lambda *refs: unpack_kernel(hosts, lanes, given, *refs),
                out_shape=shapes,
                in_specs=[vmem] * 5 + [hbm] * len(partial),
                out_specs=(hbm,) * 5,
                scratch_shapes=half_scratch,
                input_output_aliases={5 + index: index for index in range(len(partial))},
                compiler_params=params,
                name="unpack",
            )(signal, *factors, *partial)

        *outputs, grad_filter = unpack(
            True, back_given, other_factors, *unpack(False, back, own_factors)
        )
        return (*outputs, grad_filter.T)

    spec = P("context", "tensor")
    return jax.shard_map(
        local, mesh=mesh, in_specs=(spec,) * 5, out_specs=(spec,) * 5, check_vma=False
    )
```

```python
import math

import jax
import jax.numpy as jnp
import ml_dtypes
import numpy as np
from jax import lax
from jax.experimental import pallas as pl
from jax.experimental.pallas import tpu as pltpu
from jax.sharding import PartitionSpec as P

bf16 = jnp.bfloat16
f32 = jnp.float32


def split_table(table):
    high = table.astype(np.float32).astype(ml_dtypes.bfloat16)
    low = (table - high.astype(np.float64)).astype(np.float32).astype(ml_dtypes.bfloat16)
    return high, low


def tables(blocks, inner, scale):
    points = 2 * blocks * inner
    a = np.arange(blocks)
    b = np.arange(inner)
    odd = 2 * np.arange(blocks) + 1
    across = np.pi * np.outer(odd, a) / (2 * blocks)
    order = np.concatenate([np.arange(0, blocks, 2), np.arange(1, blocks, 2)])
    fore = np.concatenate([np.cos(across), -np.sin(across)], axis=0)[:, order]
    back = np.concatenate([np.cos(across), -np.sin(across)], axis=0).T
    fore_high, fore_low = split_table(fore)
    back_high, back_low = split_table(back)
    turn = np.pi * np.outer(odd, b) / points
    turn_fore = np.stack([np.cos(turn), -np.sin(turn)]).astype(np.float32)
    turn_back = (np.stack([np.cos(turn), np.sin(turn)]) * (2.0 * scale / points)).astype(np.float32)
    within = 2 * np.pi * np.outer(b, b) / inner
    cosine, sine = np.cos(within), np.sin(within)
    wide_fore = np.block([[cosine, -sine], [sine, cosine]])
    wide_back = np.block([[cosine, sine], [-sine, cosine]])
    fh, fl = split_table(wide_fore)
    bh, bl = split_table(wide_back)
    return (
        np.concatenate([fore_high, fore_high, fore_low], axis=1),
        np.block([[back_high, back_high], [back_low, np.zeros_like(back_low)]]),
        np.concatenate([fh, fl], axis=0),
        np.concatenate([bh, bl], axis=0),
        turn_fore,
        turn_back,
    )


def halves(value):
    high = value.astype(bf16)
    return high, (value - high.astype(f32)).astype(bf16)


def dot(left, right):
    return jnp.dot(left, right, preferred_element_type=f32)


def pack_rows(hosts, lanes, factors, outs, ready):
    rows = 2 * lanes + 1
    for index in range(2):
        ready(index)
        left, right = factors[2 * index], factors[2 * index + 1]
        out_ref = outs[index % len(outs)]
        stride = out_ref.shape[0] // hosts
        skip = index * lanes if stride == rows else 0
        for start in range(0, hosts * lanes, 128):
            place = pl.ds(start, 128)
            turned = (left[:, place].astype(f32) * right[:, place].astype(f32)).T
            for offset in range(0, 128, lanes):
                first = (start + offset) // lanes * stride + skip
                out_ref[pl.ds(first, lanes), :] = turned[offset : offset + lanes]


def pack_filter(hosts, part, filter_hbm, filter_ref, sem):
    rows = pl.ds(pl.multiple_of(part * hosts, hosts), hosts)
    return pltpu.make_async_copy(filter_hbm.at[rows, :], filter_ref, sem)


def pack_other_kernel(hosts, lanes, *refs):
    sources, outs, other, own, filter_ref, sems = (
        refs[:5],
        refs[5:7],
        refs[7:11],
        refs[11:15],
        refs[15],
        refs[16],
    )
    half = hosts * lanes
    core = lax.rem(lax.axis_index("context"), 2)
    copies = []
    for number, (targets, part) in enumerate(((other, 1 - core), (own, core))):
        columns = pl.ds(pl.multiple_of(part * half, half), half)
        for index in range(4):
            source = sources[index].at[:, columns]
            copies.append(
                pltpu.make_async_copy(source, targets[index], sems.at[4 * number + index])
            )
    copies.append(pack_filter(hosts, 1 - core, sources[4], filter_ref, sems.at[8]))
    for copy in copies:
        copy.start()

    def ready(index):
        copies[2 * index].wait()
        copies[2 * index + 1].wait()

    pack_rows(hosts, lanes, other, outs, ready)
    copies[8].wait()
    stride = outs[1].shape[0] // hosts
    outs[1][pl.ds(stride - 1, hosts, stride=stride), :] = filter_ref[...]
    for copy in copies[4:8]:
        copy.wait()


def pack_own_kernel(hosts, lanes, *refs):
    factors, filter_hbm, out_ref, filter_ref, sems = refs[:4], refs[4], refs[5], refs[6], refs[7]
    core = lax.rem(lax.axis_index("context"), 2)
    copy = pack_filter(hosts, core, filter_hbm, filter_ref, sems.at[0])
    copy.start()
    pack_rows(hosts, lanes, factors, (out_ref,), lambda index: None)
    copy.wait()
    stride = out_ref.shape[0] // hosts
    out_ref[pl.ds(stride - 1, hosts, stride=stride), :] = filter_ref[...]


def take_kernel(hosts, first, own_ref, out_ref):
    rows = own_ref.shape[0] // hosts
    count = out_ref.shape[0] // hosts
    for host in range(hosts):
        out_ref[pl.ds(host * count, count), :] = own_ref[pl.ds(host * rows + first, count), :]


def take_other_kernel(hosts, back_ref, out_ref):
    core = lax.rem(lax.axis_index("context"), 2)

    @pl.when(core == 0)
    def _():
        take_kernel(hosts, out_ref.shape[0] // hosts, back_ref, out_ref)

    @pl.when(core == 1)
    def _():
        take_kernel(hosts, 0, back_ref, out_ref)


def join_kernel(hosts, skipped, *refs):
    *parts, out_ref = refs
    total = out_ref.shape[0] // hosts
    for host in range(hosts):
        start = host * total
        for index, part in enumerate(parts):
            rows = part.shape[0] // hosts
            skip = 0 if index else skipped
            out_ref[pl.ds(start, rows - skip), :] = part[pl.ds(host * rows + skip, rows - skip), :]
            start += rows - skip


def convolve_kernel(
    peers,
    lanes,
    early,
    in_refs,
    fore_ref,
    back_ref,
    wide_fore_ref,
    wide_back_ref,
    turn_fore_ref,
    turn_back_ref,
    out_ref,
    high_ref,
    low_ref,
):
    rows = 2 * lanes + 1
    inner = out_ref.shape[1]
    hosts = peers // 2
    chunk = 4

    def place(first, count=1):
        return pl.ds(first * peers, count * peers)

    def put(first, value):
        high, low = halves(value)
        here = pl.ds(first * peers, value.shape[0])
        high_ref[here, :] = high
        low_ref[here, :] = low

    def transformed(first, count, table_ref):
        high = high_ref[place(first, count), :]
        low = low_ref[place(first, count), :]
        high_table = table_ref[: 2 * inner, :]
        return dot(high, high_table) + dot(low, high_table) + dot(high, table_ref[2 * inner :, :])

    def rotated(real, imag, turn_ref):
        cosine, sine = turn_ref[0], turn_ref[1]
        return jnp.concatenate(
            [real * cosine - imag * sine, real * sine + imag * cosine], axis=1
        )

    def received(row):
        if len(in_refs) == 1:
            even = in_refs[0][pl.ds(row, hosts, stride=2 * rows), :]
            odd = in_refs[0][pl.ds(rows + row, hosts, stride=2 * rows), :]
        else:
            stride = 2 * rows - early
            even = in_refs[1][pl.ds(rows - early + row, hosts, stride=stride), :]
            if row < early:
                odd = in_refs[0][pl.ds(row, hosts, stride=early), :]
            else:
                odd = in_refs[1][pl.ds(row - early, hosts, stride=stride), :]
        return jnp.concatenate([even, odd], axis=0)

    fore = fore_ref[...]
    order = [2 * lanes] + list(range(2 * lanes))
    for start in range(0, rows, 2):
        chosen = order[start : start + 2]
        columns = []
        for row in chosen:
            high, low = halves(received(row))
            columns.append(jnp.concatenate([high, low, high], axis=0))
        spread = dot(fore, jnp.concatenate(columns, axis=1))
        for index, row in enumerate(chosen):
            part = spread[:, index * inner : (index + 1) * inner]
            put(row, rotated(part[:peers], part[peers:], turn_fore_ref))

    filt = transformed(2 * lanes, 1, wide_fore_ref)
    filt_re, filt_im = filt[:, :inner], filt[:, inner:]
    corr_re = jnp.zeros((peers, inner), f32)
    corr_im = jnp.zeros((peers, inner), f32)
    for first in range(0, lanes, chunk):
        gated = transformed(first, chunk, wide_fore_ref)
        grad = transformed(lanes + first, chunk, wide_fore_ref)
        for index in range(chunk):
            part = slice(index * peers, (index + 1) * peers)
            gated_re, gated_im = gated[part, :inner], gated[part, inner:]
            grad_re, grad_im = grad[part, :inner], grad[part, inner:]
            put(
                first + index,
                jnp.concatenate(
                    [
                        gated_re * filt_re - gated_im * filt_im,
                        gated_re * filt_im + gated_im * filt_re,
                    ],
                    axis=1,
                ),
            )
            put(
                lanes + first + index,
                jnp.concatenate(
                    [
                        filt_re * grad_re + filt_im * grad_im,
                        filt_re * grad_im - filt_im * grad_re,
                    ],
                    axis=1,
                ),
            )
            corr_re = corr_re + (gated_re * grad_re + gated_im * grad_im)
            corr_im = corr_im + (gated_re * grad_im - gated_im * grad_re)
    put(2 * lanes, jnp.concatenate([corr_re, corr_im], axis=1))

    for first in range(0, rows, 3):
        count = min(3, rows - first)
        spec = transformed(first, count, wide_back_ref)
        for index in range(count):
            part = spec[index * peers : (index + 1) * peers]
            put(first + index, rotated(part[:, :inner], part[:, inner:], turn_back_ref))

    back = back_ref[...]
    for start in range(0, rows, 2):
        columns = []
        for row in range(start, min(start + 2, rows)):
            high, low = high_ref[place(row), :], low_ref[place(row), :]
            high = jnp.concatenate([high[:, :inner], high[:, inner:]], axis=0)
            low = jnp.concatenate([low[:, :inner], low[:, inner:]], axis=0)
            columns.append(jnp.concatenate([high, low], axis=0))
        signal = dot(back, jnp.concatenate(columns, axis=1))
        signal = signal[:peers] + signal[peers:]
        for index in range(len(columns)):
            out_ref[pl.ds(start + index, peers, stride=rows), :] = signal[
                :, index * inner : (index + 1) * inner
            ]


def unpack_kernel(hosts, lanes, given, *refs):
    if given:
        in_ref, *refs = refs
        refs = refs[:4] + refs[9:]
    else:
        in_ref, *refs = refs
    key_ref, value_ref, grad_ref, query_ref, *refs = refs
    targets, kept, filter_ref, sems = refs[:5], refs[5:9], refs[9], refs[10]
    rows = 2 * lanes + 1
    half = hosts * lanes
    pairs = ((query_ref, grad_ref), (value_ref, key_ref))
    core = lax.rem(lax.axis_index("context"), 2)
    part = 1 - core if given else core
    place = pl.ds(pl.multiple_of(part * half, half), half)

    def finish(first, stride):
        filter_ref[...] = in_ref[pl.ds(first + 2 * lanes, hosts, stride=stride), :]
        copies = [
            pltpu.make_async_copy(
                filter_ref,
                targets[4].at[pl.ds(pl.multiple_of(part * hosts, hosts), hosts), :],
                sems.at[4],
            )
        ]
        copies[0].start()
        for index, pair in enumerate(pairs):
            for start in range(0, half, 128):
                blocks = []
                for offset in range(0, 128, lanes):
                    row = (start + offset) // lanes * stride + first + index * lanes
                    blocks.append(in_ref[pl.ds(row, lanes), :])
                signal = jnp.concatenate(blocks, axis=0).T
                columns = pl.ds(start, 128)
                for side, factor in enumerate(pair):
                    kept[2 * index + side][:, columns] = (
                        factor[:, columns].astype(f32) * signal
                    ).astype(bf16)
            for side in range(2):
                number = 2 * index + side
                copies.append(
                    pltpu.make_async_copy(
                        kept[number], targets[number].at[:, place], sems.at[number]
                    )
                )
                copies[-1].start()
        for copy in copies:
            copy.wait()

    if given:
        finish(0, rows)
        return

    @pl.when(core == 0)
    def _():
        finish(0, 2 * rows)

    @pl.when(core == 1)
    def _():
        finish(rows, 2 * rows)


def exchange(signal, groups):
    pieces = signal.reshape(signal.shape[0], 1, signal.shape[1])
    pieces = lax.all_to_all(pieces, "context", 0, 0, axis_index_groups=groups, tiled=True)
    return pieces.reshape(signal.shape)


def solution(mesh):
    peers = mesh.shape["context"]
    hosts = peers // 2
    groups = [[2 * host + core for host in range(hosts)] for core in range(2)]
    swap = [(rank, rank ^ 1) for rank in range(peers)]
    params = pltpu.CompilerParams(vmem_limit_bytes=48 * 1024 * 1024)
    early = 4

    def local(query_gate, key_gate, value_in, filter_raw, grad_out):
        inner, width = query_gate.shape
        lanes = width // filter_raw.shape[1]
        rows = 2 * lanes + 1
        scale = 1.0 / math.sqrt(peers * inner)
        constants = [jnp.asarray(table) for table in tables(peers, inner, scale)]

        def block_rows(count):
            return jax.ShapeDtypeStruct((hosts * count, inner), f32)

        held_half = pltpu.VMEM((inner, width // 2), bf16)
        half_scratch = [held_half] * 4 + [
            pltpu.VMEM((hosts, inner), f32),
            pltpu.SemaphoreType.DMA((5,)),
        ]
        half_wide = jax.ShapeDtypeStruct((inner, width // 2), bf16)
        sources = [
            pltpu.with_memory_space_constraint(array, pltpu.HBM)
            for array in (key_gate, value_in, grad_out, query_gate, filter_raw.T)
        ]

        hbm = pl.BlockSpec(memory_space=pltpu.HBM)
        vmem = pl.BlockSpec(memory_space=pltpu.VMEM)
        filter_half = pltpu.VMEM((hosts, inner), f32)
        other_gated, other_grad, *factors = pl.pallas_call(
            lambda *refs: pack_other_kernel(hosts, lanes, *refs),
            out_shape=(block_rows(lanes), block_rows(lanes + 1)) + (half_wide,) * 8,
            in_specs=[hbm] * 5,
            scratch_shapes=[filter_half, pltpu.SemaphoreType.DMA((9,))],
            compiler_params=params,
            name="pack_other",
        )(*sources)
        other_factors, own_factors = factors[:4], factors[4:]
        given_gated = lax.ppermute(other_gated, "context", swap)
        given_grad = lax.ppermute(other_grad, "context", swap)
        own = pl.pallas_call(
            lambda *refs: pack_own_kernel(hosts, lanes, *refs),
            out_shape=block_rows(rows),
            in_specs=[vmem] * 4 + [hbm],
            scratch_shapes=[filter_half, pltpu.SemaphoreType.DMA((1,))],
            compiler_params=params,
            name="pack_own",
        )(*own_factors, sources[4])

        def convolve(*held):
            count = len(held)
            return pl.pallas_call(
                lambda *refs: convolve_kernel(peers, lanes, early, refs[:count], *refs[count:]),
                out_shape=block_rows(2 * rows),
                scratch_shapes=[pltpu.VMEM((peers * rows, 2 * inner), bf16)] * 2,
                compiler_params=params,
                name="convolve",
            )(*held, *constants)

        def join(kernel, size, *parts):
            return pl.pallas_call(
                kernel, out_shape=block_rows(size), compiler_params=params, name="join"
            )(*parts)

        leads = lax.rem(lax.axis_index("context"), 2) == 0
        def lead(*parts):
            sent = join(lambda *refs: join_kernel(hosts, 0, *refs), 2 * rows, *parts)
            return exchange(convolve(exchange(sent, groups)), groups)

        def follow(own, *given):
            ahead = join(lambda *refs: take_kernel(hosts, 0, *refs), early, own)
            sent = join(
                lambda *refs: join_kernel(hosts, early, *refs), 2 * rows - early, own, *given
            )
            held_ahead, sent = lax.optimization_barrier((exchange(ahead, groups), sent))
            return exchange(convolve(held_ahead, exchange(sent, groups)), groups)

        back = lax.cond(leads, lead, follow, own, given_gated, given_grad)
        other_back = join(lambda *refs: take_other_kernel(hosts, *refs), rows, back)
        back_given = lax.ppermute(other_back, "context", swap)
        wide = jax.ShapeDtypeStruct((inner, width), bf16)
        shapes = (wide,) * 4 + (jax.ShapeDtypeStruct((peers, inner), f32),)
        hbm = pl.BlockSpec(memory_space=pltpu.HBM)
        vmem = pl.BlockSpec(memory_space=pltpu.VMEM)

        def unpack(given, signal, factors, *partial):
            return pl.pallas_call(
                lambda *refs: unpack_kernel(hosts, lanes, given, *refs),
                out_shape=shapes,
                in_specs=[vmem] * 5 + [hbm] * len(partial),
                out_specs=(hbm,) * 5,
                scratch_shapes=half_scratch,
                input_output_aliases={5 + index: index for index in range(len(partial))},
                compiler_params=params,
                name="unpack",
            )(signal, *factors, *partial)

        *outputs, grad_filter = unpack(
            True, back_given, other_factors, *unpack(False, back, own_factors)
        )
        return (*outputs, grad_filter.T)

    spec = P("context", "tensor")
    return jax.shard_map(
        local, mesh=mesh, in_specs=(spec,) * 5, out_specs=(spec,) * 5, check_vma=False
    )
```
